256 devices in a mesh: rows: 32 (over y, x, core), cols: 8 (over z).
Axes of the slice: x: 4, y: 4, z: 8, core: 2. Of those that a mesh axis runs over, the one named last changes fastest.
Arguments:
- samples: float32 [2, 16384, 4096], P(None, 'rows', 'cols'), may hold values from -6 to 6
- sketch: float32 [2, 4096, 256], P(None, 'cols'), may hold values from -0.0625 to 0.0625
Outputs:
- basis: float32 [2, 16384, 512], P(None, 'rows')
- projected: float32 [2, 512, 4096], P(None, None, 'cols')
The draws below stay inside these ranges and needn't reach their ends.
All inputs are finite; a program needn't handle non-finite values.
Results may differ from the reference program's by a relative error of at most 0.000088.
Values sent between devices are 32-bit elements; how exact they have to be, the bound alone decides.
A program may use at most 64 MiB of HBM per device.

```python
import jax
import jax.numpy as jnp
from jax import lax

N = 4096
K = 256
M = 16384


def draw_samples(key, part):
    key = jax.random.fold_in(key, 11)
    key_main = jax.random.fold_in(key, 0)
    values = jnp.clip(jax.random.normal(key_main, (2, M, N), jnp.float32), -6.0, 6.0)
    return values.astype(jnp.float32)


def shard_levels(stream_key, shape, cuts, smallest, top_value):
    def one(dim, parts):
        heights = jax.random.uniform(jax.random.fold_in(jax.random.fold_in(stream_key, 6), dim), (parts,), jnp.float32, smallest / len(cuts), top_value / len(cuts))
        return jnp.repeat(jnp.exp(heights), shape[dim] // parts).reshape((-1,) + (1,) * (len(shape) - dim - 1))

    level = one(*cuts[0])
    for cut in cuts[1:]:
        level = level * one(*cut)
    return level


def normal_values(key, extent, scale, bound, cuts=(), dtype=jnp.bfloat16):
    drawn = jax.random.normal(key, extent, jnp.float32) * scale
    if len(cuts) > 0:
        drawn = shard_levels(key, extent, cuts, -0.22, 0.18) * drawn
    return jnp.clip(drawn, min=-bound, max=bound).astype(dtype)


def setup_inputs(seed: int = 0) -> dict:
    arg_keys = jax.random.split(jax.random.key(seed), 3)
    samples = draw_samples(jax.random.fold_in(arg_keys[2], 71), 0)
    sketch = normal_values(arg_keys[1], (2, N, K), (2 * N) ** -0.5, 0.0625, ((1, 8),), jnp.float32)
    return {"samples": samples, "sketch": sketch}


HI = lax.Precision.HIGHEST

def mult(left, right):
    return jnp.dot(left.astype(jnp.float32), right.astype(jnp.float32), precision=HI, preferred_element_type=jnp.float32)

def mult_t(left, right):
    return lax.dot_general(left.astype(jnp.float32), right.astype(jnp.float32), (((0,), (0,)), ((), ())), precision=HI, preferred_element_type=jnp.float32)

def reference(samples, sketch):
    real_a, imag_a = (samples[0], samples[1])
    real_s, imag_s = (sketch[0], sketch[1])
    first_r = mult(real_a, real_s) - mult(imag_a, imag_s)
    first_i = mult(real_a, imag_s) + mult(imag_a, real_s)
    back_r = mult_t(real_a, first_r) + mult_t(imag_a, first_i)
    back_i = mult_t(real_a, first_i) - mult_t(imag_a, first_r)
    power_r = mult(real_a, back_r) - mult(imag_a, back_i)
    power_i = mult(real_a, back_i) + mult(imag_a, back_r)
    gram_r = mult_t(power_r, power_r) + mult_t(power_i, power_i)
    gram_i = mult_t(power_r, power_i) - mult_t(power_i, power_r)
    gram = jnp.concatenate([jnp.concatenate([gram_r, -gram_i], 1), jnp.concatenate([gram_i, gram_r], 1)], 0)
    lower = jnp.linalg.cholesky(gram)
    upper_rows = jnp.concatenate([power_r, -power_i], 1)
    lower_rows = jnp.concatenate([power_i, power_r], 1)
    basis_top = lax.linalg.triangular_solve(lower, upper_rows, left_side=False, lower=True, transpose_a=True)
    basis_bot = lax.linalg.triangular_solve(lower, lower_rows, left_side=False, lower=True, transpose_a=True)
    left_half = mult_t(basis_top, real_a) + mult_t(basis_bot, imag_a)
    right_half = mult_t(basis_bot, real_a) - mult_t(basis_top, imag_a)
    scale = jnp.sqrt(jnp.float32(2 * M))
    basis = jnp.stack([basis_top, basis_bot]) * scale
    return (basis, jnp.stack([left_half, right_half]))
```

```python
import functools

import jax
import jax.numpy as jnp
from jax import lax
from jax.experimental import pallas as pl
from jax.experimental.pallas import tpu as pltpu
from jax.sharding import PartitionSpec as P

MESH = pl.DeviceIdType.MESH
HI = lax.Precision.HIGHEST
F32 = jnp.float32
BF16 = jnp.bfloat16

Z_SLOTS = 28
ROW_SLOTS = 34
GRAM_SLOTS = 21


def split(value):
    high = value.astype(BF16)
    return high, (value - high.astype(F32)).astype(BF16)


class Copies:
    def __init__(self, send_sem, recv_sem):
        self.send_sem, self.recv_sem = send_sem, recv_sem
        self.made = {}

    def send(self, slot, src, dst, device):
        copy = pltpu.make_async_remote_copy(
            src_ref=src, dst_ref=dst, send_sem=self.send_sem.at[slot],
            recv_sem=self.recv_sem.at[slot], device_id=device, device_id_type=MESH,
        )
        copy.start()
        self.made[slot] = copy

    def arrived(self, slot):
        self.made[slot].wait_recv()

    def finish(self):
        for copy in self.made.values():
            copy.wait_send()


class Place:
    def __init__(self):
        self.r = lax.axis_index("rows")
        self.z = lax.axis_index("cols")
        self.core = lax.rem(self.r, 2)
        self.x = lax.rem(self.r // 2, 4)
        self.y = self.r // 8

    def along_z(self, d):
        return (self.r, lax.rem(self.z + d + 8, 8))

    def along_x(self, d):
        return ((self.y * 4 + lax.rem(self.x + d, 4)) * 2 + self.core, self.z)

    def along_y(self, d):
        return ((lax.rem(self.y + d, 4) * 4 + self.x) * 2 + self.core, self.z)

    def sibling(self):
        return (self.r + 1 - 2 * self.core, self.z)

    def line(self, axis, d):
        return self.along_x(d) if axis == 0 else self.along_y(d)

    def at(self, axis):
        return self.x if axis == 0 else self.y


def greet(place):
    barrier = pltpu.get_barrier_semaphore()
    peers = [place.sibling()]
    peers += [place.along_x(d) for d in (1, 2, 3)]
    peers += [place.along_y(d) for d in (1, 2, 3)]
    peers += [place.along_z(d) for d in range(1, 8)]
    for peer in peers:
        pl.semaphore_signal(barrier, inc=1, device_id=peer, device_id_type=MESH)
    pl.semaphore_wait(barrier, len(peers))


def wrap8(value):
    return lax.rem(value + 16, 8)


class RingZ:
    def __init__(self, place, copies, base, part, slots, full):
        self.place, self.copies, self.base = place, copies, base
        self.part, self.slots, self.full = part, slots, full

    def scatter_steps(self):
        place, copies, part, slots = self.place, self.copies, self.part, self.slots

        def slot(way, half, dist):
            return self.base + (0 if way > 0 else 7) + (dist - 1 if half == lead(way) else 3 + dist)

        def lead(way):
            return 0 if way > 0 else 1

        def box(way, half, dist):
            return (0 if way > 0 else 7) + (dist - 1 if half == lead(way) else 3 + dist)

        def push(way, half, dist):
            chunk = wrap8(place.z + way * dist)
            copies.send(slot(way, half, dist), part.at[chunk, half], slots.at[box(way, half, dist)],
                        place.along_z(way))

        def pull(way, half, dist):
            copies.arrived(slot(way, half, dist))
            chunk = wrap8(place.z + way * (dist - 1))
            part[chunk, half] = part[chunk, half] + slots[box(way, half, dist)]

        for way in (1, -1):
            push(way, lead(way), 4)
        for way in (1, -1):
            push(way, 1 - lead(way), 3)
        yield
        for step in range(3):
            for way in (1, -1):
                half = lead(way)
                pull(way, half, 4 - step)
                push(way, half, 3 - step)
            for way in (1, -1):
                half = 1 - lead(way)
                pull(way, half, 3 - step)
                if step < 2:
                    push(way, half, 2 - step)
            yield
        for way in (1, -1):
            pull(way, lead(way), 1)
        yield

    def gather_steps(self):
        place, copies, full, part = self.place, self.copies, self.full, self.part
        me = place.z
        full[me] = part[me]
        base = self.base + 14

        def slot(way, half, dist):
            return base + (0 if way > 0 else 7) + (dist * 2 + half if dist < 3 else 6)

        def push(way, half, dist):
            chunk = wrap8(me - way * dist)
            ref = full.at[chunk, half]
            copies.send(slot(way, half, dist), ref, ref, place.along_z(way))

        for half in (0, 1):
            for way in (1, -1):
                push(way, half, 0)
        yield
        for dist in (1, 2):
            for half in (0, 1):
                for way in (1, -1):
                    copies.arrived(slot(way, half, dist - 1))
                    push(way, half, dist)
            yield
        for half in (0, 1):
            for way in (1, -1):
                copies.arrived(slot(way, half, 2))
                if half == (0 if way > 0 else 1):
                    push(way, half, 3)
        yield
        for way in (1, -1):
            copies.arrived(slot(way, 0 if way > 0 else 1, 3))
        yield


class SumRows:
    def __init__(self, place, copies, base, part, from_core, from_line, from_point, full):
        self.place, self.copies, self.base = place, copies, base
        self.part, self.full = part, full
        self.from_core, self.from_line, self.from_point = from_core, from_line, from_point

    def steps(self):
        place, copies, base = self.place, self.copies, self.base
        part, full, core = self.part, self.full, place.core
        first = [place.at(0), place.at(1)]
        second = [place.at(1), place.at(0)]
        for h in (0, 1):
            copies.send(base + h, part.at[h, 1 - core], self.from_core.at[h], place.sibling())
        yield
        base += 2
        for h in (0, 1):
            copies.arrived(base - 2 + h)
            for d in (2, 1, 3):
                at = lax.rem(first[h] + d, 4)
                part[h, core, at] = part[h, core, at] + self.from_core[h, at]
                copies.send(base + 3 * h + d - 1, part.at[h, core, at], self.from_line.at[h, d - 1],
                            place.line(h, d))
            at = first[h]
            part[h, core, at] = part[h, core, at] + self.from_core[h, at]
        yield
        base += 6
        for h in (0, 1):
            a = first[h]
            for d in (1, 2, 3):
                copies.arrived(base - 6 + 3 * h + d - 1)
            part[h, core, a] = (part[h, core, a] + self.from_line[h, 0]) + (
                self.from_line[h, 1] + self.from_line[h, 2])
            for d in (2, 1, 3):
                b = lax.rem(second[h] + d, 4)
                copies.send(base + 3 * h + d - 1, part.at[h, core, a, b], self.from_point.at[h, d - 1],
                            place.line(1 - h, d))
        yield
        base += 6
        for h in (0, 1):
            a, b = first[h], second[h]
            for d in (1, 2, 3):
                copies.arrived(base - 6 + 3 * h + d - 1)
            full[h, core, a, b] = (part[h, core, a, b] + self.from_point[h, 0]) + (
                self.from_point[h, 1] + self.from_point[h, 2])
            for d in (2, 1, 3):
                ref = full.at[h, core, a, b]
                copies.send(base + 3 * h + d - 1, ref, ref, place.line(1 - h, d))
        yield
        base += 6
        for h in (0, 1):
            a = first[h]
            for d in (1, 2, 3):
                copies.arrived(base - 6 + 3 * h + d - 1)
            ref = full.at[h, core, a]
            for d in (2, 1, 3):
                copies.send(base + 3 * h + d - 1, ref, ref, place.line(h, d))
            copies.send(base + 6 + 4 * h, ref, ref, place.sibling())
        yield
        for h in (0, 1):
            for d in (1, 3, 2):
                copies.arrived(base + 3 * h + d - 1)
                ref = full.at[h, core, lax.rem(first[h] - d + 4, 4)]
                copies.send(base + 6 + 4 * h + d, ref, ref, place.sibling())
        yield
        for h in (0, 1):
            for d in range(4):
                copies.arrived(base + 6 + 4 * h + d)
        yield


class SumAll:
    def __init__(self, place, copies, base, part, from_core, from_line, from_point, from_z, full):
        self.place, self.copies, self.base = place, copies, base
        self.part, self.full = part, full
        self.from_core, self.from_line, self.from_point, self.from_z = (
            from_core, from_line, from_point, from_z)

    def steps(self):
        place, copies, base = self.place, self.copies, self.base
        part, full, core, x, y = self.part, self.full, place.core, place.x, place.y
        copies.send(base, part.at[1 - core], self.from_core, place.sibling())
        yield
        copies.arrived(base)
        base += 1
        part[core] = part[core] + self.from_core[...]
        for d in (2, 1, 3):
            copies.send(base + d - 1, part.at[core, lax.rem(x + d, 4)], self.from_line.at[d - 1],
                        place.along_x(d))
        yield
        for d in (1, 2, 3):
            copies.arrived(base + d - 1)
        base += 3
        part[core, x] = (part[core, x] + self.from_line[0]) + (self.from_line[1] + self.from_line[2])
        for d in (2, 1, 3):
            copies.send(base + d - 1, part.at[core, x, lax.rem(y + d, 4)], self.from_point.at[d - 1],
                        place.along_y(d))
        yield
        for d in (1, 2, 3):
            copies.arrived(base + d - 1)
        base += 3
        mine = self.from_z.at[place.z]
        mine[...] = (part[core, x, y] + self.from_point[0]) + (self.from_point[1] + self.from_point[2])
        for d in (4, 3, 5, 2, 6, 1, 7):
            copies.send(base + d - 1, mine, mine, place.along_z(d))
        yield
        for d in range(1, 8):
            copies.arrived(base + d - 1)
        base += 7
        total = self.from_z[0]
        for z in range(1, 8):
            total = total + self.from_z[z]
        full[core, x, y] = total
        ref = full.at[core, x, y]
        for d in (2, 1, 3):
            copies.send(base + d - 1, ref, ref, place.along_y(d))
        yield
        for d in (1, 2, 3):
            copies.arrived(base + d - 1)
        base += 3
        ref = full.at[core, x]
        for d in (2, 1, 3):
            copies.send(base + d - 1, ref, ref, place.along_x(d))
        yield
        for d in (1, 2, 3):
            copies.arrived(base + d - 1)
        base += 3
        ref = full.at[core]
        copies.send(base, ref, ref, place.sibling())
        yield
        copies.arrived(base)
        yield


def run(steps):
    for _ in steps:
        pass


def interleave(*many):
    live = list(many)
    while live:
        live = [one for one in live if next(one, run) is None]


def multiply(x_hi, x_lo, t_hi, t_lo, store):
    def tile(i, j):
        rows, lanes = pl.ds(i * 256, 256), pl.ds(j * 256, 256)
        xh, xl = x_hi[rows, :], x_lo[rows, :]
        th, tl = t_hi[:, lanes], t_lo[:, lanes]
        dot = functools.partial(jnp.dot, preferred_element_type=F32)
        store(i, j, dot(xh, th) + (dot(xh, tl) + dot(xl, th)))

    @pl.loop(0, 2)
    def _(i):
        for j in range(2):
            tile(i, j)


def power_kernel(a_ref, s_ref, y_ref, b_ref, g_ref, x_hi, x_lo, xt_hi, xt_lo, t_hi, t_lo,
                 z_part, z_slots, z_full, z_part2, z_slots2,
                 r_part, r_core, r_line, r_point, r_full, r_part2, r_core2, r_line2, r_point2,
                 g_part, g_core, g_line, g_point, g_z, send_sem, recv_sem):
    place = Place()
    greet(place)
    copies = Copies(send_sem, recv_sem)

    def set_pair(rows, real, imag, sign):
        low = pl.ds(rows, real.shape[0])
        high = pl.ds(512 + rows, real.shape[0])
        for at, lanes, value in (
            (low, slice(0, 256), real), (low, slice(256, 512), imag),
            (high, slice(0, 256), sign * imag), (high, slice(256, 512), -sign * real),
        ):
            t_hi[at, lanes], t_lo[at, lanes] = split(value)

    @pl.loop(0, 8)
    def _(i):
        rows = pl.ds(i * 64, 64)
        for p in (0, 1):
            x_hi[rows, p * 512:(p + 1) * 512], x_lo[rows, p * 512:(p + 1) * 512] = split(a_ref[p, rows, :])
        set_pair(i * 64, s_ref[0, rows, :], s_ref[1, rows, :], -1.0)

    def store_chunks(ref):
        def store(i, j, tile):
            ref[pl.ds(i * 4, 4), :, :, j * 256:(j + 1) * 256] = tile.reshape(4, 2, 32, 256)
        return store

    def store_rows(ref):
        def store(i, j, tile):
            ref[j, i] = tile.reshape(4, 4, 16, 256)
        return store

    multiply(x_hi, x_lo, t_hi, t_lo, store_chunks(z_part))
    ring = RingZ(place, copies, 0, z_part, z_slots, z_full)
    steps = ring.scatter_steps()
    next(steps)

    @pl.loop(0, 4)
    def _(i):
        for p in (0, 1):
            rows = pl.ds(i * 128, 128)
            block = a_ref[p, :, rows].T
            lanes = slice(p * 512, (p + 1) * 512)
            xt_hi[rows, lanes], xt_lo[rows, lanes] = split(block)

    run(steps)
    run(ring.gather_steps())

    def chunks_to_t(ref):
        @pl.loop(0, 8)
        def _(i):
            value = ref[i].reshape(64, 512)
            set_pair(i * 64, value[:, :256], value[:, 256:], 1.0)

    chunks_to_t(z_full)
    multiply(xt_hi, xt_lo, t_hi, t_lo, store_rows(r_part))
    run(SumRows(place, copies, Z_SLOTS, r_part, r_core, r_line, r_point, r_full).steps())

    for k in (0, 1):
        @pl.loop(0, 4)
        def _(i):
            set_pair(k * 256 + i * 64, r_full[0, k, i].reshape(64, 256), r_full[1, k, i].reshape(64, 256), -1.0)

    multiply(x_hi, x_lo, t_hi, t_lo, store_chunks(z_part2))
    ring = RingZ(place, copies, Z_SLOTS + ROW_SLOTS, z_part2, z_slots2, y_ref)
    run(ring.scatter_steps())
    mine = z_part2[place.z].reshape(64, 512)
    steps = ring.gather_steps()
    next(steps)
    real, imag = mine[:, :256], mine[:, 256:]
    tall = jnp.concatenate([real, imag], 0).T
    gram_r = jnp.dot(tall, jnp.concatenate([real, imag], 0), precision=HI, preferred_element_type=F32)
    gram_i = jnp.dot(tall, jnp.concatenate([imag, -real], 0), precision=HI, preferred_element_type=F32)
    low = lax.broadcasted_iota(jnp.int32, (256, 256), 0) >= lax.broadcasted_iota(jnp.int32, (256, 256), 1)
    g_part[...] = jnp.where(low, gram_r, gram_i).reshape(2, 4, 4, 8, 256)
    gram_steps = SumAll(place, copies, 2 * Z_SLOTS + ROW_SLOTS, g_part, g_core, g_line, g_point, g_z, g_ref).steps()
    interleave(gram_steps, steps)

    chunks_to_t(y_ref)
    multiply(xt_hi, xt_lo, t_hi, t_lo, store_rows(r_part2))
    run(SumRows(place, copies, 2 * Z_SLOTS + ROW_SLOTS + GRAM_SLOTS, r_part2, r_core2, r_line2, r_point2,
                b_ref).steps())
    copies.finish()


def power(samples, sketch):
    vmem = pl.BlockSpec(memory_space=pltpu.VMEM)
    slots = 2 * Z_SLOTS + 2 * ROW_SLOTS + GRAM_SLOTS
    chunks = pltpu.VMEM((8, 2, 32, 512), F32)
    boxes = pltpu.VMEM((14, 32, 512), F32)
    rows = [
        pltpu.VMEM((2, 2, 4, 4, 16, 256), F32),
        pltpu.VMEM((2, 4, 4, 16, 256), F32),
        pltpu.VMEM((2, 3, 4, 16, 256), F32),
        pltpu.VMEM((2, 3, 16, 256), F32),
    ]
    return pl.pallas_call(
        power_kernel,
        out_shape=(
            jax.ShapeDtypeStruct((8, 2, 32, 512), F32),
            jax.ShapeDtypeStruct((2, 2, 4, 4, 16, 256), F32),
            jax.ShapeDtypeStruct((2, 4, 4, 8, 256), F32),
        ),
        in_specs=[vmem] * 2,
        out_specs=(vmem,) * 3,
        scratch_shapes=[
            *[pltpu.VMEM((512, 1024), BF16)] * 4,
            *[pltpu.VMEM((1024, 512), BF16)] * 2,
            chunks, boxes, chunks, chunks, boxes,
            *rows, pltpu.VMEM((2, 2, 4, 4, 16, 256), F32), *rows,
            pltpu.VMEM((2, 4, 4, 8, 256), F32),
            pltpu.VMEM((4, 4, 8, 256), F32),
            pltpu.VMEM((3, 4, 8, 256), F32),
            pltpu.VMEM((3, 8, 256), F32),
            pltpu.VMEM((8, 8, 256), F32),
            pltpu.SemaphoreType.DMA((slots,)),
            pltpu.SemaphoreType.DMA((slots,)),
        ],
        compiler_params=pltpu.CompilerParams(
            collective_id=0, has_side_effects=True, vmem_limit_bytes=48 * 2**20
        ),
        name="power",
    )(samples, sketch)


def mult(left, right):
    return jnp.dot(left, right, precision=HI, preferred_element_type=F32)


def per_device(samples, sketch):
    y, b, packed = power(samples, sketch)
    y = y.reshape(512, 512)
    b = b.reshape(2, 512, 256)
    packed = packed.reshape(256, 256)
    gram_r = jnp.tril(packed) + jnp.tril(packed, -1).T
    gram_i = jnp.triu(packed, 1) - jnp.triu(packed, 1).T
    gram = jnp.concatenate(
        [jnp.concatenate([gram_r, -gram_i], 1), jnp.concatenate([gram_i, gram_r], 1)], 0
    )
    lower = jnp.linalg.cholesky(gram)
    inverse = lax.linalg.triangular_solve(lower, jnp.eye(512, dtype=F32), left_side=True, lower=True)
    yr, yi = y[:, :256], y[:, 256:]
    total_rows = samples.shape[1] * lax.axis_size("rows")
    scale = jnp.sqrt(jnp.float32(2 * total_rows))
    top = mult(jnp.concatenate([yr, -yi], 1), inverse.T)
    bot = mult(jnp.concatenate([yi, yr], 1), inverse.T)
    basis = jnp.stack([top, bot]) * scale
    projected = jnp.stack([
        mult(inverse, jnp.concatenate([b[0], -b[1]], 1).T),
        mult(inverse, jnp.concatenate([b[1], b[0]], 1).T),
    ])
    return (basis, projected)


def solution(mesh):
    placed = (P(None, "rows", "cols"), P(None, "cols", None))
    return jax.shard_map(
        per_device,
        mesh=mesh,
        in_specs=placed,
        out_specs=(P(None, "rows", None), P(None, None, "cols")),
        check_vma=False,
    )
```

```python
import functools

import jax
import jax.numpy as jnp
import numpy as np
from jax import lax
from jax.experimental import pallas as pl
from jax.experimental.pallas import tpu as pltpu
from jax.sharding import PartitionSpec as P

MESH = pl.DeviceIdType.MESH
HI = lax.Precision.HIGHEST
F32 = jnp.float32
BF16 = jnp.bfloat16

Z_SLOTS = 28
ROW_SLOTS = 34
GRAM_SLOTS = 21


def split(value):
    high = value.astype(BF16)
    return high, (value - high.astype(F32)).astype(BF16)


class Copies:
    def __init__(self, send_sem, recv_sem):
        self.send_sem, self.recv_sem = send_sem, recv_sem
        self.made = {}

    def send(self, slot, src, dst, device):
        copy = pltpu.make_async_remote_copy(
            src_ref=src, dst_ref=dst, send_sem=self.send_sem.at[slot],
            recv_sem=self.recv_sem.at[slot], device_id=device, device_id_type=MESH,
        )
        copy.start()
        self.made[slot] = copy

    def arrived(self, slot):
        self.made[slot].wait_recv()

    def finish(self):
        for copy in self.made.values():
            copy.wait_send()


class Place:
    def __init__(self):
        self.r = lax.axis_index("rows")
        self.z = lax.axis_index("cols")
        self.core = lax.rem(self.r, 2)
        self.x = lax.rem(self.r // 2, 4)
        self.y = self.r // 8

    def along_z(self, d):
        return (self.r, lax.rem(self.z + d + 8, 8))

    def along_x(self, d):
        return ((self.y * 4 + lax.rem(self.x + d, 4)) * 2 + self.core, self.z)

    def along_y(self, d):
        return ((lax.rem(self.y + d, 4) * 4 + self.x) * 2 + self.core, self.z)

    def sibling(self):
        return (self.r + 1 - 2 * self.core, self.z)

    def line(self, axis, d):
        return self.along_x(d) if axis == 0 else self.along_y(d)

    def at(self, axis):
        return self.x if axis == 0 else self.y


def greet(place):
    barrier = pltpu.get_barrier_semaphore()
    peers = [place.sibling()]
    peers += [place.along_x(d) for d in (1, 2, 3)]
    peers += [place.along_y(d) for d in (1, 2, 3)]
    peers += [place.along_z(d) for d in range(1, 8)]
    for peer in peers:
        pl.semaphore_signal(barrier, inc=1, device_id=peer, device_id_type=MESH)
    pl.semaphore_wait(barrier, len(peers))


def wrap8(value):
    return lax.rem(value + 16, 8)


class RingZ:
    def __init__(self, place, copies, base, part, slots, full):
        self.place, self.copies, self.base = place, copies, base
        self.part, self.slots, self.full = part, slots, full

    def scatter_steps(self):
        place, copies, part, slots = self.place, self.copies, self.part, self.slots

        def slot(way, half, dist):
            return self.base + (0 if way > 0 else 7) + (dist - 1 if half == lead(way) else 3 + dist)

        def lead(way):
            return 0 if way > 0 else 1

        def box(way, half, dist):
            return (0 if way > 0 else 7) + (dist - 1 if half == lead(way) else 3 + dist)

        def push(way, half, dist):
            chunk = wrap8(place.z + way * dist)
            copies.send(slot(way, half, dist), part.at[chunk, half], slots.at[box(way, half, dist)],
                        place.along_z(way))

        def pull(way, half, dist):
            copies.arrived(slot(way, half, dist))
            chunk = wrap8(place.z + way * (dist - 1))
            part[chunk, half] = part[chunk, half] + slots[box(way, half, dist)]

        for way in (1, -1):
            push(way, lead(way), 4)
        for way in (1, -1):
            push(way, 1 - lead(way), 3)
        yield
        for step in range(3):
            for way in (1, -1):
                half = lead(way)
                pull(way, half, 4 - step)
                push(way, half, 3 - step)
            for way in (1, -1):
                half = 1 - lead(way)
                pull(way, half, 3 - step)
                if step < 2:
                    push(way, half, 2 - step)
            yield
        for way in (1, -1):
            pull(way, lead(way), 1)
        yield

    def gather_steps(self):
        place, copies, full, part = self.place, self.copies, self.full, self.part
        me = place.z
        full[me] = part[me]
        base = self.base + 14

        def slot(way, half, dist):
            return base + (0 if way > 0 else 7) + (dist * 2 + half if dist < 3 else 6)

        def push(way, half, dist):
            chunk = wrap8(me - way * dist)
            ref = full.at[chunk, half]
            copies.send(slot(way, half, dist), ref, ref, place.along_z(way))

        for half in (0, 1):
            for way in (1, -1):
                push(way, half, 0)
        yield
        for dist in (1, 2):
            for half in (0, 1):
                for way in (1, -1):
                    copies.arrived(slot(way, half, dist - 1))
                    push(way, half, dist)
            yield
        for half in (0, 1):
            for way in (1, -1):
                copies.arrived(slot(way, half, 2))
                if half == (0 if way > 0 else 1):
                    push(way, half, 3)
        yield
        for way in (1, -1):
            copies.arrived(slot(way, 0 if way > 0 else 1, 3))
        yield


class SumRows:
    def __init__(self, place, copies, base, part, from_core, from_line, from_point, full):
        self.place, self.copies, self.base = place, copies, base
        self.part, self.full = part, full
        self.from_core, self.from_line, self.from_point = from_core, from_line, from_point

    def steps(self):
        place, copies, base = self.place, self.copies, self.base
        part, full, core = self.part, self.full, place.core
        first = [place.at(0), place.at(1)]
        second = [place.at(1), place.at(0)]
        for h in (0, 1):
            copies.send(base + h, part.at[h, 1 - core], self.from_core.at[h], place.sibling())
        yield
        base += 2
        for h in (0, 1):
            copies.arrived(base - 2 + h)
            for d in (2, 1, 3):
                at = lax.rem(first[h] + d, 4)
                part[h, core, at] = part[h, core, at] + self.from_core[h, at]
                copies.send(base + 3 * h + d - 1, part.at[h, core, at], self.from_line.at[h, d - 1],
                            place.line(h, d))
            at = first[h]
            part[h, core, at] = part[h, core, at] + self.from_core[h, at]
        yield
        base += 6
        for h in (0, 1):
            a = first[h]
            for d in (1, 2, 3):
                copies.arrived(base - 6 + 3 * h + d - 1)
            part[h, core, a] = (part[h, core, a] + self.from_line[h, 0]) + (
                self.from_line[h, 1] + self.from_line[h, 2])
            for d in (2, 1, 3):
                b = lax.rem(second[h] + d, 4)
                copies.send(base + 3 * h + d - 1, part.at[h, core, a, b], self.from_point.at[h, d - 1],
                            place.line(1 - h, d))
        yield
        base += 6
        for h in (0, 1):
            a, b = first[h], second[h]
            for d in (1, 2, 3):
                copies.arrived(base - 6 + 3 * h + d - 1)
            full[h, core, a, b] = (part[h, core, a, b] + self.from_point[h, 0]) + (
                self.from_point[h, 1] + self.from_point[h, 2])
            for d in (2, 1, 3):
                ref = full.at[h, core, a, b]
                copies.send(base + 3 * h + d - 1, ref, ref, place.line(1 - h, d))
        yield
        base += 6
        for h in (0, 1):
            a = first[h]
            for d in (1, 2, 3):
                copies.arrived(base - 6 + 3 * h + d - 1)
            ref = full.at[h, core, a]
            for d in (2, 1, 3):
                copies.send(base + 3 * h + d - 1, ref, ref, place.line(h, d))
            copies.send(base + 6 + 4 * h, ref, ref, place.sibling())
        yield
        for h in (0, 1):
            for d in (1, 3, 2):
                copies.arrived(base + 3 * h + d - 1)
                ref = full.at[h, core, lax.rem(first[h] - d + 4, 4)]
                copies.send(base + 6 + 4 * h + d, ref, ref, place.sibling())
        yield
        for h in (0, 1):
            for d in range(4):
                copies.arrived(base + 6 + 4 * h + d)
        yield


class SumAll:
    def __init__(self, place, copies, base, part, from_core, from_line, from_point, from_z, full):
        self.place, self.copies, self.base = place, copies, base
        self.part, self.full = part, full
        self.from_core, self.from_line, self.from_point, self.from_z = (
            from_core, from_line, from_point, from_z)

    def steps(self):
        place, copies, base = self.place, self.copies, self.base
        part, full, core, x, y = self.part, self.full, place.core, place.x, place.y
        copies.send(base, part.at[1 - core], self.from_core, place.sibling())
        yield
        copies.arrived(base)
        base += 1
        part[core] = part[core] + self.from_core[...]
        for d in (2, 1, 3):
            copies.send(base + d - 1, part.at[core, lax.rem(x + d, 4)], self.from_line.at[d - 1],
                        place.along_x(d))
        yield
        for d in (1, 2, 3):
            copies.arrived(base + d - 1)
        base += 3
        part[core, x] = (part[core, x] + self.from_line[0]) + (self.from_line[1] + self.from_line[2])
        for d in (2, 1, 3):
            copies.send(base + d - 1, part.at[core, x, lax.rem(y + d, 4)], self.from_point.at[d - 1],
                        place.along_y(d))
        yield
        for d in (1, 2, 3):
            copies.arrived(base + d - 1)
        base += 3
        mine = self.from_z.at[place.z]
        mine[...] = (part[core, x, y] + self.from_point[0]) + (self.from_point[1] + self.from_point[2])
        for d in (4, 3, 5, 2, 6, 1, 7):
            copies.send(base + d - 1, mine, mine, place.along_z(d))
        yield
        for d in range(1, 8):
            copies.arrived(base + d - 1)
        base += 7
        total = self.from_z[0]
        for z in range(1, 8):
            total = total + self.from_z[z]
        full[core, x, y] = total
        ref = full.at[core, x, y]
        for d in (2, 1, 3):
            copies.send(base + d - 1, ref, ref, place.along_y(d))
        yield
        for d in (1, 2, 3):
            copies.arrived(base + d - 1)
        base += 3
        ref = full.at[core, x]
        for d in (2, 1, 3):
            copies.send(base + d - 1, ref, ref, place.along_x(d))
        yield
        for d in (1, 2, 3):
            copies.arrived(base + d - 1)
        base += 3
        ref = full.at[core]
        copies.send(base, ref, ref, place.sibling())
        yield
        copies.arrived(base)
        yield


def run(steps):
    for _ in steps:
        pass


def interleave(*many):
    live = list(many)
    while live:
        live = [one for one in live if next(one, run) is None]


def multiply(x_hi, x_lo, t_hi, t_lo, store):
    def tile(i, j):
        rows, lanes = pl.ds(i * 256, 256), pl.ds(j * 256, 256)
        xh, xl = x_hi[rows, :], x_lo[rows, :]
        th, tl = t_hi[:, lanes], t_lo[:, lanes]
        dot = functools.partial(jnp.dot, preferred_element_type=F32)
        store(i, j, dot(xh, th) + (dot(xh, tl) + dot(xl, th)))

    @pl.loop(0, 2)
    def _(i):
        for j in range(2):
            tile(i, j)


def power_kernel(a_ref, s_ref, y_ref, b_ref, g_ref, x_hi, x_lo, xt_hi, xt_lo, t_hi, t_lo,
                 z_part, z_slots, z_full, z_part2, z_slots2,
                 r_part, r_core, r_line, r_point, r_full, r_part2, r_core2, r_line2, r_point2,
                 g_part, g_core, g_line, g_point, g_z, send_sem, recv_sem):
    place = Place()
    greet(place)
    copies = Copies(send_sem, recv_sem)

    def set_pair(rows, real, imag, sign):
        low = pl.ds(rows, real.shape[0])
        high = pl.ds(512 + rows, real.shape[0])
        for at, lanes, value in (
            (low, slice(0, 256), real), (low, slice(256, 512), imag),
            (high, slice(0, 256), sign * imag), (high, slice(256, 512), -sign * real),
        ):
            t_hi[at, lanes], t_lo[at, lanes] = split(value)

    @pl.loop(0, 8)
    def _(i):
        rows = pl.ds(i * 64, 64)
        for p in (0, 1):
            x_hi[rows, p * 512:(p + 1) * 512], x_lo[rows, p * 512:(p + 1) * 512] = split(a_ref[p, rows, :])
        set_pair(i * 64, s_ref[0, rows, :], s_ref[1, rows, :], -1.0)

    def store_chunks(ref):
        def store(i, j, tile):
            ref[pl.ds(i * 4, 4), :, :, j * 256:(j + 1) * 256] = tile.reshape(4, 2, 32, 256)
        return store

    def store_rows(ref):
        def store(i, j, tile):
            ref[j, i] = tile.reshape(4, 4, 16, 256)
        return store

    multiply(x_hi, x_lo, t_hi, t_lo, store_chunks(z_part))
    ring = RingZ(place, copies, 0, z_part, z_slots, z_full)
    steps = ring.scatter_steps()
    next(steps)

    @pl.loop(0, 4)
    def _(i):
        for p in (0, 1):
            rows = pl.ds(i * 128, 128)
            block = a_ref[p, :, rows].T
            lanes = slice(p * 512, (p + 1) * 512)
            xt_hi[rows, lanes], xt_lo[rows, lanes] = split(block)

    run(steps)
    run(ring.gather_steps())

    def chunks_to_t(ref):
        @pl.loop(0, 8)
        def _(i):
            value = ref[i].reshape(64, 512)
            set_pair(i * 64, value[:, :256], value[:, 256:], 1.0)

    chunks_to_t(z_full)
    multiply(xt_hi, xt_lo, t_hi, t_lo, store_rows(r_part))
    run(SumRows(place, copies, Z_SLOTS, r_part, r_core, r_line, r_point, r_full).steps())

    for k in (0, 1):
        @pl.loop(0, 4)
        def _(i):
            set_pair(k * 256 + i * 64, r_full[0, k, i].reshape(64, 256), r_full[1, k, i].reshape(64, 256), -1.0)

    multiply(x_hi, x_lo, t_hi, t_lo, store_chunks(z_part2))
    ring = RingZ(place, copies, Z_SLOTS + ROW_SLOTS, z_part2, z_slots2, y_ref)
    run(ring.scatter_steps())
    mine = z_part2[place.z].reshape(64, 512)
    steps = ring.gather_steps()
    next(steps)
    real, imag = mine[:, :256], mine[:, 256:]
    tall = jnp.concatenate([real, imag], 0).T
    gram_r = jnp.dot(tall, jnp.concatenate([real, imag], 0), precision=HI, preferred_element_type=F32)
    gram_i = jnp.dot(tall, jnp.concatenate([imag, -real], 0), precision=HI, preferred_element_type=F32)
    low = lax.broadcasted_iota(jnp.int32, (256, 256), 0) >= lax.broadcasted_iota(jnp.int32, (256, 256), 1)
    g_part[...] = jnp.where(low, gram_r, gram_i).reshape(2, 4, 4, 8, 256)
    gram_steps = SumAll(place, copies, 2 * Z_SLOTS + ROW_SLOTS, g_part, g_core, g_line, g_point, g_z, g_ref).steps()
    interleave(gram_steps, steps)

    chunks_to_t(y_ref)
    multiply(xt_hi, xt_lo, t_hi, t_lo, store_rows(r_part2))
    run(SumRows(place, copies, 2 * Z_SLOTS + ROW_SLOTS + GRAM_SLOTS, r_part2, r_core2, r_line2, r_point2,
                b_ref).steps())
    copies.finish()


def power(samples, sketch):
    vmem = pl.BlockSpec(memory_space=pltpu.VMEM)
    slots = 2 * Z_SLOTS + 2 * ROW_SLOTS + GRAM_SLOTS
    chunks = pltpu.VMEM((8, 2, 32, 512), F32)
    boxes = pltpu.VMEM((14, 32, 512), F32)
    rows = [
        pltpu.VMEM((2, 2, 4, 4, 16, 256), F32),
        pltpu.VMEM((2, 4, 4, 16, 256), F32),
        pltpu.VMEM((2, 3, 4, 16, 256), F32),
        pltpu.VMEM((2, 3, 16, 256), F32),
    ]
    return pl.pallas_call(
        power_kernel,
        out_shape=(
            jax.ShapeDtypeStruct((8, 2, 32, 512), F32),
            jax.ShapeDtypeStruct((2, 2, 4, 4, 16, 256), F32),
            jax.ShapeDtypeStruct((2, 4, 4, 8, 256), F32),
        ),
        in_specs=[vmem] * 2,
        out_specs=(vmem,) * 3,
        scratch_shapes=[
            *[pltpu.VMEM((512, 1024), BF16)] * 4,
            *[pltpu.VMEM((1024, 512), BF16)] * 2,
            chunks, boxes, chunks, chunks, boxes,
            *rows, pltpu.VMEM((2, 2, 4, 4, 16, 256), F32), *rows,
            pltpu.VMEM((2, 4, 4, 8, 256), F32),
            pltpu.VMEM((4, 4, 8, 256), F32),
            pltpu.VMEM((3, 4, 8, 256), F32),
            pltpu.VMEM((3, 8, 256), F32),
            pltpu.VMEM((8, 8, 256), F32),
            pltpu.SemaphoreType.DMA((slots,)),
            pltpu.SemaphoreType.DMA((slots,)),
        ],
        compiler_params=pltpu.CompilerParams(
            collective_id=0, has_side_effects=True, vmem_limit_bytes=48 * 2**20
        ),
        name="power",
    )(samples, sketch)


def inverse2(a, b, c):
    r = 1.0 / (a * c - b * b)
    return c * r, -(b * r), a * r


def dots(lefts, rights):
    total = lefts[0] * rights[0]
    for left, right in zip(lefts[1:], rights[1:]):
        total = total + left * right
    return total


def inverse_sym(p):
    n = len(p)
    if n == 2:
        a, b, c = inverse2(p[0][0], p[0][1], p[1][1])
        return [[a, b], [b, c]]
    h = n // 2
    top = inverse_sym([row[:h] for row in p[:h]])
    cross = [row[h:] for row in p[:h]]
    t, s = eliminate(top, cross, [row[h:] for row in p[h:]])
    low = inverse_sym(s)
    x = [[-dots(t[i], low[j]) for j in range(h)] for i in range(h)]
    first = [[None] * h for _ in range(h)]
    for i in range(h):
        for j in range(i, h):
            first[i][j] = first[j][i] = top[i][j] - dots(x[i], t[j])
    return [first[i] + x[i] for i in range(h)] + [[x[i][j] for i in range(h)] + low[j] for j in range(h)]


def eliminate(top, cross, corner):
    h = len(top)
    t = [[dots(top[i], [cross[k][j] for k in range(h)]) for j in range(h)] for i in range(h)]
    s = [[None] * h for _ in range(h)]
    for i in range(h):
        for j in range(i, h):
            s[i][j] = s[j][i] = corner[i][j] - dots([cross[k][i] for k in range(h)], [t[k][j] for k in range(h)])
    return t, s


def inverse_factor(ref, start):
    groups = [ref[start + 8 * g:start + 8 * g + 8, start:start + 128] for g in range(16)]
    lane = lax.broadcasted_iota(jnp.int32, (8, 128), 1)
    sub = lax.broadcasted_iota(jnp.int32, (8, 128), 0)
    wide = (8, 128)
    for g in range(16):
        own = groups[g]
        at = 8 * g
        inside = (lane >= at) & (lane < at + 8)
        rows = [jnp.broadcast_to(own[k:k + 1, :], wide) for k in range(8)]
        if g < 15:
            p = [[None] * 8 for _ in range(8)]
            for i in range(8):
                for j in range(i, 8):
                    p[i][j] = p[j][i] = jnp.broadcast_to(rows[i][:, at + j:at + j + 1], wide)
            unit = [jnp.where(inside, jnp.where(lane == at + k, 1.0, 0.0), rows[k]) for k in range(8)]
            top = inverse_sym([row[:4] for row in p[:4]])
            t, s = eliminate(top, [row[4:] for row in p[:4]], [row[4:] for row in p[4:]])
            low = inverse_sym(s)
            rest = [unit[4 + j] - dots([t[i][j] for i in range(4)], unit[:4]) for j in range(4)]
            q_low = [dots(low[j], rest) for j in range(4)]
            q_top = [dots(top[i], unit[:4]) - dots(t[i], q_low) for i in range(4)]
            q = q_top + q_low
            for v in range(g + 1, 16):
                cols = [jnp.broadcast_to(groups[v][:, at + k:at + k + 1], wide) for k in range(8)]
                base = jnp.where(inside, 0.0, groups[v])
                groups[v] = base - ((dots(cols[:2], q[:2]) + dots(cols[2:4], q[2:4]))
                                    + (dots(cols[4:6], q[4:6]) + dots(cols[6:], q[6:])))
        for k in range(8):
            row = jnp.broadcast_to(own[k:k + 1, :], wide)
            pivot = jnp.broadcast_to(row[:, at + k:at + k + 1], wide)
            inv = 1.0 / pivot
            col = jnp.broadcast_to(own[:, at + k:at + k + 1], wide)
            base = jnp.where(lane == at + k, 0.0, own)
            row = jnp.where(lane == at + k, 1.0, row)
            own = jnp.where(sub > k, base - col * (row * inv), jnp.where(sub == k, row * lax.rsqrt(pivot), own))
        ref[start + at:start + at + 8, start:start + 128] = jnp.where(lane <= at + sub, own, 0.0)


def factor(m_ref):
    dot = functools.partial(jnp.dot, precision=HI, preferred_element_type=F32)
    for k in range(4):
        at = 128 * k
        inverse_factor(m_ref, at)
        w = m_ref[at:at + 128, at:at + 128]
        if k > 0:
            m_ref[at:at + 128, :at] = dot(w, m_ref[at:at + 128, :at])
        if k < 3:
            u = dot(w, m_ref[at:at + 128, at + 128:])
            ut = u.T
            m_ref[at + 128:, at + 128:] = m_ref[at + 128:, at + 128:] - dot(ut, u)
            if k > 0:
                m_ref[at + 128:, :at] = m_ref[at + 128:, :at] - dot(ut, m_ref[at:at + 128, :at])
            m_ref[at + 128:, at:at + 128] = -dot(ut, w)
            m_ref[at:at + 128, at + 128:] = jnp.zeros((128, 384 - at), F32)


def finish_kernel(scale, y_ref, b_ref, g_ref, basis_ref, proj_ref, m_ref, l_hi, l_lo):
    packed = g_ref[...]
    row = lax.broadcasted_iota(jnp.int32, (256, 256), 0)
    col = lax.broadcasted_iota(jnp.int32, (256, 256), 1)
    turned = packed.T
    gram_r = jnp.where(row >= col, packed, turned)
    gram_i = jnp.where(row < col, packed, jnp.where(row > col, -turned, 0.0))
    m_ref[:256, :256] = gram_r
    m_ref[256:, 256:] = gram_r
    m_ref[256:, :256] = gram_i
    m_ref[:256, 256:] = -gram_i
    factor(m_ref)
    for i in range(4):
        rows = slice(128 * i, 128 * i + 128)
        l_hi[rows, :], l_lo[rows, :] = split(m_ref[rows, :])

    def product(left_hi, left_lo, right_hi, right_lo):
        dot = functools.partial(
            lax.dot_general, dimension_numbers=(((1,), (1,)), ((), ())), preferred_element_type=F32)
        return dot(left_hi, right_hi) + (dot(left_hi, right_lo) + dot(left_lo, right_hi))

    @pl.loop(0, 2)
    def _(i):
        rows = pl.ds(i * 256, 256)
        real, imag = y_ref[rows, :256], y_ref[rows, 256:]
        basis_ref[0, rows, :] = product(*split(jnp.concatenate([real, -imag], 1)), l_hi[...], l_lo[...]) * scale
        basis_ref[1, rows, :] = product(*split(jnp.concatenate([imag, real], 1)), l_hi[...], l_lo[...]) * scale

    @pl.loop(0, 2)
    def _(i):
        rows = pl.ds(i * 256, 256)
        real, imag = b_ref[0], b_ref[1]
        hi, lo = l_hi[rows, :], l_lo[rows, :]
        proj_ref[0, rows, :] = product(hi, lo, *split(jnp.concatenate([real, -imag], 1)))
        proj_ref[1, rows, :] = product(hi, lo, *split(jnp.concatenate([imag, real], 1)))


def finish(y, b, packed, scale):
    vmem = pl.BlockSpec(memory_space=pltpu.VMEM)
    return pl.pallas_call(
        functools.partial(finish_kernel, scale),
        out_shape=(jax.ShapeDtypeStruct((2, 512, 512), F32),) * 2,
        in_specs=[vmem] * 3,
        out_specs=(vmem,) * 2,
        scratch_shapes=[
            pltpu.VMEM((512, 512), F32),
            pltpu.VMEM((512, 512), BF16),
            pltpu.VMEM((512, 512), BF16),
        ],
        compiler_params=pltpu.CompilerParams(vmem_limit_bytes=48 * 2**20),
        name="finish",
    )(y, b, packed)


def per_device(samples, sketch):
    y, b, packed = power(samples, sketch)
    total_rows = samples.shape[1] * lax.axis_size("rows")
    scale = float(np.sqrt(np.float32(2 * total_rows)))
    return finish(y.reshape(512, 512), b.reshape(2, 512, 256), packed.reshape(256, 256), scale)


def solution(mesh):
    placed = (P(None, "rows", "cols"), P(None, "cols", None))
    return jax.shard_map(
        per_device,
        mesh=mesh,
        in_specs=placed,
        out_specs=(P(None, "rows", None), P(None, None, "cols")),
        check_vma=False,
    )
```

```python
import functools

import jax
import jax.numpy as jnp
import numpy as np
from jax import lax
from jax.experimental import pallas as pl
from jax.experimental.pallas import tpu as pltpu
from jax.sharding import PartitionSpec as P

MESH = pl.DeviceIdType.MESH
HI = lax.Precision.HIGHEST
F32 = jnp.float32
BF16 = jnp.bfloat16

Z_SLOTS = 28
ROW_SLOTS = 34
GRAM_SLOTS = 21


def split(value):
    high = value.astype(BF16)
    return high, (value - high.astype(F32)).astype(BF16)


class Copies:
    def __init__(self, send_sem, recv_sem):
        self.send_sem, self.recv_sem = send_sem, recv_sem
        self.made = {}

    def send(self, slot, src, dst, device):
        copy = pltpu.make_async_remote_copy(
            src_ref=src, dst_ref=dst, send_sem=self.send_sem.at[slot],
            recv_sem=self.recv_sem.at[slot], device_id=device, device_id_type=MESH,
        )
        copy.start()
        self.made[slot] = copy

    def arrived(self, slot):
        self.made[slot].wait_recv()

    def finish(self):
        for copy in self.made.values():
            copy.wait_send()


class Place:
    def __init__(self):
        self.r = lax.axis_index("rows")
        self.z = lax.axis_index("cols")
        self.core = lax.rem(self.r, 2)
        self.x = lax.rem(self.r // 2, 4)
        self.y = self.r // 8

    def along_z(self, d):
        return (self.r, lax.rem(self.z + d + 8, 8))

    def along_x(self, d):
        return ((self.y * 4 + lax.rem(self.x + d, 4)) * 2 + self.core, self.z)

    def along_y(self, d):
        return ((lax.rem(self.y + d, 4) * 4 + self.x) * 2 + self.core, self.z)

    def sibling(self):
        return (self.r + 1 - 2 * self.core, self.z)

    def line(self, axis, d):
        return self.along_x(d) if axis == 0 else self.along_y(d)

    def at(self, axis):
        return self.x if axis == 0 else self.y


def greet(place):
    barrier = pltpu.get_barrier_semaphore()
    peers = [place.sibling()]
    peers += [place.along_x(d) for d in (1, 2, 3)]
    peers += [place.along_y(d) for d in (1, 2, 3)]
    peers += [place.along_z(d) for d in range(1, 8)]
    for peer in peers:
        pl.semaphore_signal(barrier, inc=1, device_id=peer, device_id_type=MESH)
    pl.semaphore_wait(barrier, len(peers))


def wrap8(value):
    return lax.rem(value + 16, 8)


class RingZ:
    def __init__(self, place, copies, base, part, slots, full):
        self.place, self.copies, self.base = place, copies, base
        self.part, self.slots, self.full = part, slots, full

    def scatter_steps(self):
        place, copies, part, slots = self.place, self.copies, self.part, self.slots

        def slot(way, half, dist):
            return self.base + (0 if way > 0 else 7) + (dist - 1 if half == lead(way) else 3 + dist)

        def lead(way):
            return 0 if way > 0 else 1

        def box(way, half, dist):
            return (0 if way > 0 else 7) + (dist - 1 if half == lead(way) else 3 + dist)

        def push(way, half, dist):
            chunk = wrap8(place.z + way * dist)
            copies.send(slot(way, half, dist), part.at[chunk, half], slots.at[box(way, half, dist)],
                        place.along_z(way))

        def pull(way, half, dist):
            copies.arrived(slot(way, half, dist))
            chunk = wrap8(place.z + way * (dist - 1))
            part[chunk, half] = part[chunk, half] + slots[box(way, half, dist)]

        for way in (1, -1):
            push(way, lead(way), 4)
        for way in (1, -1):
            push(way, 1 - lead(way), 3)
        yield
        for step in range(3):
            for way in (1, -1):
                half = lead(way)
                pull(way, half, 4 - step)
                push(way, half, 3 - step)
            for way in (1, -1):
                half = 1 - lead(way)
                pull(way, half, 3 - step)
                if step < 2:
                    push(way, half, 2 - step)
            yield
        for way in (1, -1):
            pull(way, lead(way), 1)
        yield

    def gather_steps(self):
        place, copies, full, part = self.place, self.copies, self.full, self.part
        me = place.z
        full[me] = part[me]
        base = self.base + 14

        def slot(way, half, dist):
            return base + (0 if way > 0 else 7) + (dist * 2 + half if dist < 3 else 6)

        def push(way, half, dist):
            chunk = wrap8(me - way * dist)
            ref = full.at[chunk, half]
            copies.send(slot(way, half, dist), ref, ref, place.along_z(way))

        for half in (0, 1):
            for way in (1, -1):
                push(way, half, 0)
        yield
        for dist in (1, 2):
            for half in (0, 1):
                for way in (1, -1):
                    copies.arrived(slot(way, half, dist - 1))
                    push(way, half, dist)
            yield
        for half in (0, 1):
            for way in (1, -1):
                copies.arrived(slot(way, half, 2))
                if half == (0 if way > 0 else 1):
                    push(way, half, 3)
        yield
        for way in (1, -1):
            copies.arrived(slot(way, 0 if way > 0 else 1, 3))
        yield


class SumRows:
    def __init__(self, place, copies, base, part, from_core, from_line, from_point, full):
        self.place, self.copies, self.base = place, copies, base
        self.part, self.full = part, full
        self.from_core, self.from_line, self.from_point = from_core, from_line, from_point

    def steps(self):
        place, copies, base = self.place, self.copies, self.base
        part, full, core = self.part, self.full, place.core
        first = [place.at(0), place.at(1)]
        second = [place.at(1), place.at(0)]
        for h in (0, 1):
            copies.send(base + h, part.at[h, 1 - core], self.from_core.at[h], place.sibling())
        yield
        base += 2
        for h in (0, 1):
            copies.arrived(base - 2 + h)
            for d in (2, 1, 3):
                at = lax.rem(first[h] + d, 4)
                part[h, core, at] = part[h, core, at] + self.from_core[h, at]
                copies.send(base + 3 * h + d - 1, part.at[h, core, at], self.from_line.at[h, d - 1],
                            place.line(h, d))
            at = first[h]
            part[h, core, at] = part[h, core, at] + self.from_core[h, at]
        yield
        base += 6
        for h in (0, 1):
            a = first[h]
            for d in (1, 2, 3):
                copies.arrived(base - 6 + 3 * h + d - 1)
            part[h, core, a] = (part[h, core, a] + self.from_line[h, 0]) + (
                self.from_line[h, 1] + self.from_line[h, 2])
            for d in (2, 1, 3):
                b = lax.rem(second[h] + d, 4)
                copies.send(base + 3 * h + d - 1, part.at[h, core, a, b], self.from_point.at[h, d - 1],
                            place.line(1 - h, d))
        yield
        base += 6
        for h in (0, 1):
            a, b = first[h], second[h]
            for d in (1, 2, 3):
                copies.arrived(base - 6 + 3 * h + d - 1)
            full[h, core, a, b] = (part[h, core, a, b] + self.from_point[h, 0]) + (
                self.from_point[h, 1] + self.from_point[h, 2])
            for d in (2, 1, 3):
                ref = full.at[h, core, a, b]
                copies.send(base + 3 * h + d - 1, ref, ref, place.line(1 - h, d))
        yield
        base += 6
        for h in (0, 1):
            a = first[h]
            for d in (1, 2, 3):
                copies.arrived(base - 6 + 3 * h + d - 1)
            ref = full.at[h, core, a]
            for d in (2, 1, 3):
                copies.send(base + 3 * h + d - 1, ref, ref, place.line(h, d))
            copies.send(base + 6 + 4 * h, ref, ref, place.sibling())
        yield
        for h in (0, 1):
            for d in (1, 3, 2):
                copies.arrived(base + 3 * h + d - 1)
                ref = full.at[h, core, lax.rem(first[h] - d + 4, 4)]
                copies.send(base + 6 + 4 * h + d, ref, ref, place.sibling())
        yield
        for h in (0, 1):
            for d in range(4):
                copies.arrived(base + 6 + 4 * h + d)
        yield


class SumAll:
    def __init__(self, place, copies, base, part, from_core, from_line, from_point, from_z, full):
        self.place, self.copies, self.base = place, copies, base
        self.part, self.full = part, full
        self.from_core, self.from_line, self.from_point, self.from_z = (
            from_core, from_line, from_point, from_z)

    def steps(self):
        place, copies, base = self.place, self.copies, self.base
        part, full, core, x, y = self.part, self.full, place.core, place.x, place.y
        copies.send(base, part.at[1 - core], self.from_core, place.sibling())
        yield
        copies.arrived(base)
        base += 1
        part[core] = part[core] + self.from_core[...]
        for d in (2, 1, 3):
            copies.send(base + d - 1, part.at[core, lax.rem(x + d, 4)], self.from_line.at[d - 1],
                        place.along_x(d))
        yield
        for d in (1, 2, 3):
            copies.arrived(base + d - 1)
        base += 3
        part[core, x] = (part[core, x] + self.from_line[0]) + (self.from_line[1] + self.from_line[2])
        for d in (2, 1, 3):
            copies.send(base + d - 1, part.at[core, x, lax.rem(y + d, 4)], self.from_point.at[d - 1],
                        place.along_y(d))
        yield
        for d in (1, 2, 3):
            copies.arrived(base + d - 1)
        base += 3
        mine = self.from_z.at[place.z]
        mine[...] = (part[core, x, y] + self.from_point[0]) + (self.from_point[1] + self.from_point[2])
        for d in (4, 3, 5, 2, 6, 1, 7):
            copies.send(base + d - 1, mine, mine, place.along_z(d))
        yield
        for d in range(1, 8):
            copies.arrived(base + d - 1)
        base += 7
        total = self.from_z[0]
        for z in range(1, 8):
            total = total + self.from_z[z]
        full[core, x, y] = total
        ref = full.at[core, x, y]
        for d in (2, 1, 3):
            copies.send(base + d - 1, ref, ref, place.along_y(d))
        yield
        for d in (1, 2, 3):
            copies.arrived(base + d - 1)
        base += 3
        ref = full.at[core, x]
        for d in (2, 1, 3):
            copies.send(base + d - 1, ref, ref, place.along_x(d))
        yield
        for d in (1, 2, 3):
            copies.arrived(base + d - 1)
        base += 3
        ref = full.at[core]
        copies.send(base, ref, ref, place.sibling())
        yield
        copies.arrived(base)
        yield


def run(steps):
    for _ in steps:
        pass


def interleave(*many):
    live = list(many)
    while live:
        live = [one for one in live if next(one, run) is None]


def multiply(x_hi, x_lo, t_hi, t_lo, store):
    def tile(i, j):
        rows, lanes = pl.ds(i * 256, 256), pl.ds(j * 256, 256)
        xh, xl = x_hi[rows, :], x_lo[rows, :]
        th, tl = t_hi[:, lanes], t_lo[:, lanes]
        dot = functools.partial(jnp.dot, preferred_element_type=F32)
        store(i, j, dot(xh, th) + (dot(xh, tl) + dot(xl, th)))

    @pl.loop(0, 2)
    def _(i):
        for j in range(2):
            tile(i, j)


def dots(lefts, rights):
    terms = [left * right for left, right in zip(lefts, rights)]
    while len(terms) > 1:
        terms = [sum(terms[i + 1:i + 2], terms[i]) for i in range(0, len(terms), 2)]
    return terms[0]


def inverse_factor(ref, start, hook):
    groups = [ref[start + 8 * g:start + 8 * g + 8, start:start + 128] for g in range(16)]
    wide = (8, 128)
    lane = lax.broadcasted_iota(jnp.int32, wide, 1)
    sub = lax.broadcasted_iota(jnp.int32, wide, 0)

    def row(value, k):
        return jnp.broadcast_to(value[k:k + 1, :], wide)

    def col(value, k):
        return jnp.broadcast_to(value[:, k:k + 1], wide)

    for g in range(16):
        at = 8 * g
        inside = (lane >= at) & (lane < at + 8)
        own = groups[g]
        c = [col(own, at + k) for k in range(8)]
        u = jnp.where(inside, jnp.where(lane == at + sub, 1.0, 0.0), own)
        inverse = root = jnp.zeros(wide, F32)
        for k in range(8):
            pivot = row(c[k], k)
            inv = 1.0 / pivot
            inverse = jnp.where(sub == k, inv, inverse)
            root = jnp.where(sub == k, lax.rsqrt(pivot), root)
            if k < 7:
                f = jnp.where(sub > k, c[k], 0.0) * inv
                for m in range(k + 1, 8):
                    c[m] = c[m] - f * row(c[m], k)
                u = u - f * row(u, k)
        ref[start + at:start + at + 8, start:start + 128] = jnp.where(lane <= at + sub, u * root, 0.0)
        hook((start + at) // 8)
        if g == 15:
            break
        q = u * inverse
        for m in range(7, 0, -1):
            q = q - jnp.where(sub < m, c[m] * inverse, 0.0) * row(q, m)
        rows = [row(q, k) for k in range(8)]
        for v in range(g + 1, 16):
            cols = [col(groups[v], at + k) for k in range(8)]
            groups[v] = jnp.where(inside, 0.0, groups[v]) - dots(cols, rows)


def factor(m_ref, hook):
    dot = functools.partial(jnp.dot, precision=HI, preferred_element_type=F32)
    for k in range(4):
        at = 128 * k
        inverse_factor(m_ref, at, hook)
        w = m_ref[at:at + 128, at:at + 128]
        if k > 0:
            m_ref[at:at + 128, :at] = dot(w, m_ref[at:at + 128, :at])
        if k < 3:
            u = dot(w, m_ref[at:at + 128, at + 128:])
            ut = u.T
            m_ref[at + 128:, at + 128:] = m_ref[at + 128:, at + 128:] - dot(ut, u)
            if k > 0:
                m_ref[at + 128:, :at] = m_ref[at + 128:, :at] - dot(ut, m_ref[at:at + 128, :at])
            m_ref[at + 128:, at:at + 128] = -dot(ut, w)
            m_ref[at:at + 128, at + 128:] = jnp.zeros((128, 384 - at), F32)


def set_gram(packed, m_ref):
    row = lax.broadcasted_iota(jnp.int32, (256, 256), 0)
    col = lax.broadcasted_iota(jnp.int32, (256, 256), 1)
    turned = packed.T
    gram_r = jnp.where(row >= col, packed, turned)
    gram_i = jnp.where(row < col, packed, jnp.where(row > col, -turned, 0.0))
    m_ref[:256, :256] = gram_r
    m_ref[256:, 256:] = gram_r
    m_ref[256:, :256] = gram_i
    m_ref[:256, 256:] = -gram_i


def finish_kernel(scale, y_ref, b_ref, m_ref, basis_ref, proj_ref, l_hi, l_lo):
    for i in range(4):
        rows = slice(128 * i, 128 * i + 128)
        l_hi[rows, :], l_lo[rows, :] = split(m_ref[rows, :])

    def product(left_hi, left_lo, right_hi, right_lo):
        dot = functools.partial(
            lax.dot_general, dimension_numbers=(((1,), (1,)), ((), ())), preferred_element_type=F32)
        return dot(left_hi, right_hi) + (dot(left_hi, right_lo) + dot(left_lo, right_hi))

    @pl.loop(0, 2)
    def _(i):
        rows = pl.ds(i * 256, 256)
        real, imag = y_ref[rows, :256], y_ref[rows, 256:]
        basis_ref[0, rows, :] = product(*split(jnp.concatenate([real, -imag], 1)), l_hi[...], l_lo[...]) * scale
        basis_ref[1, rows, :] = product(*split(jnp.concatenate([imag, real], 1)), l_hi[...], l_lo[...]) * scale

    @pl.loop(0, 2)
    def _(i):
        rows = pl.ds(i * 256, 256)
        real, imag = b_ref[0], b_ref[1]
        hi, lo = l_hi[rows, :], l_lo[rows, :]
        proj_ref[0, rows, :] = product(hi, lo, *split(jnp.concatenate([real, -imag], 1)))
        proj_ref[1, rows, :] = product(hi, lo, *split(jnp.concatenate([imag, real], 1)))


def finish(y, b, inverse, scale):
    vmem = pl.BlockSpec(memory_space=pltpu.VMEM)
    return pl.pallas_call(
        functools.partial(finish_kernel, scale),
        out_shape=(jax.ShapeDtypeStruct((2, 512, 512), F32),) * 2,
        in_specs=[vmem] * 3,
        out_specs=(vmem,) * 2,
        scratch_shapes=[
            pltpu.VMEM((512, 512), BF16),
            pltpu.VMEM((512, 512), BF16),
        ],
        compiler_params=pltpu.CompilerParams(vmem_limit_bytes=48 * 2**20),
        name="finish",
    )(y, b, inverse)

HOOKS = (0, 4, 11, 18, 25, 33, 41, 50)


def power_kernel(a_ref, s_ref, y_ref, b_ref, m_ref, x_hi, x_lo, xt_hi, xt_lo, t_hi, t_lo,
                 z_part, z_slots, z_full, z_part2, z_slots2,
                 r_part, r_core, r_line, r_point, r_full, r_part2, r_core2, r_line2, r_point2,
                 g_ref, g_part, g_core, g_line, g_point, g_z, send_sem, recv_sem):
    place = Place()
    greet(place)
    copies = Copies(send_sem, recv_sem)

    def set_pair(rows, real, imag, sign):
        low = pl.ds(rows, real.shape[0])
        high = pl.ds(512 + rows, real.shape[0])
        for at, lanes, value in (
            (low, slice(0, 256), real), (low, slice(256, 512), imag),
            (high, slice(0, 256), sign * imag), (high, slice(256, 512), -sign * real),
        ):
            t_hi[at, lanes], t_lo[at, lanes] = split(value)

    @pl.loop(0, 8)
    def _(i):
        rows = pl.ds(i * 64, 64)
        for p in (0, 1):
            x_hi[rows, p * 512:(p + 1) * 512], x_lo[rows, p * 512:(p + 1) * 512] = split(a_ref[p, rows, :])
        set_pair(i * 64, s_ref[0, rows, :], s_ref[1, rows, :], -1.0)

    def store_chunks(ref):
        def store(i, j, tile):
            ref[pl.ds(i * 4, 4), :, :, j * 256:(j + 1) * 256] = tile.reshape(4, 2, 32, 256)
        return store

    def store_rows(ref):
        def store(i, j, tile):
            ref[j, i] = tile.reshape(4, 4, 16, 256)
        return store

    multiply(x_hi, x_lo, t_hi, t_lo, store_chunks(z_part))
    ring = RingZ(place, copies, 0, z_part, z_slots, z_full)
    steps = ring.scatter_steps()
    next(steps)

    @pl.loop(0, 4)
    def _(i):
        for p in (0, 1):
            rows = pl.ds(i * 128, 128)
            block = a_ref[p, :, rows].T
            lanes = slice(p * 512, (p + 1) * 512)
            xt_hi[rows, lanes], xt_lo[rows, lanes] = split(block)

    run(steps)
    run(ring.gather_steps())

    def chunks_to_t(ref):
        @pl.loop(0, 8)
        def _(i):
            value = ref[i].reshape(64, 512)
            set_pair(i * 64, value[:, :256], value[:, 256:], 1.0)

    chunks_to_t(z_full)
    multiply(xt_hi, xt_lo, t_hi, t_lo, store_rows(r_part))
    run(SumRows(place, copies, Z_SLOTS, r_part, r_core, r_line, r_point, r_full).steps())

    for k in (0, 1):
        @pl.loop(0, 4)
        def _(i):
            set_pair(k * 256 + i * 64, r_full[0, k, i].reshape(64, 256), r_full[1, k, i].reshape(64, 256), -1.0)

    multiply(x_hi, x_lo, t_hi, t_lo, store_chunks(z_part2))
    ring = RingZ(place, copies, Z_SLOTS + ROW_SLOTS, z_part2, z_slots2, y_ref)
    run(ring.scatter_steps())
    mine = z_part2[place.z].reshape(64, 512)
    steps = ring.gather_steps()
    next(steps)
    real, imag = mine[:, :256], mine[:, 256:]
    tall = jnp.concatenate([real, imag], 0).T
    gram_r = jnp.dot(tall, jnp.concatenate([real, imag], 0), precision=HI, preferred_element_type=F32)
    gram_i = jnp.dot(tall, jnp.concatenate([imag, -real], 0), precision=HI, preferred_element_type=F32)
    low = lax.broadcasted_iota(jnp.int32, (256, 256), 0) >= lax.broadcasted_iota(jnp.int32, (256, 256), 1)
    g_part[...] = jnp.where(low, gram_r, gram_i).reshape(2, 4, 4, 8, 256)
    gram_steps = SumAll(place, copies, 2 * Z_SLOTS + ROW_SLOTS, g_part, g_core, g_line, g_point, g_z, g_ref).steps()
    for _ in range(4):
        next(gram_steps)
    next(steps)
    next(gram_steps)
    next(steps)
    next(gram_steps)
    next(steps)
    run(gram_steps)

    def behind():
        run(steps)
        chunks_to_t(y_ref)
        multiply(xt_hi, xt_lo, t_hi, t_lo, store_rows(r_part2))
        yield
        yield from SumRows(place, copies, 2 * Z_SLOTS + ROW_SLOTS + GRAM_SLOTS, r_part2, r_core2, r_line2,
                           r_point2, b_ref).steps()

    rest = behind()

    def hook(done):
        if done in HOOKS:
            next(rest)

    set_gram(g_ref[...].reshape(256, 256), m_ref)
    factor(m_ref, hook)
    run(rest)
    copies.finish()


def power(samples, sketch):
    vmem = pl.BlockSpec(memory_space=pltpu.VMEM)
    slots = 2 * Z_SLOTS + 2 * ROW_SLOTS + GRAM_SLOTS
    chunks = pltpu.VMEM((8, 2, 32, 512), F32)
    boxes = pltpu.VMEM((14, 32, 512), F32)
    rows = [
        pltpu.VMEM((2, 2, 4, 4, 16, 256), F32),
        pltpu.VMEM((2, 4, 4, 16, 256), F32),
        pltpu.VMEM((2, 3, 4, 16, 256), F32),
        pltpu.VMEM((2, 3, 16, 256), F32),
    ]
    return pl.pallas_call(
        power_kernel,
        out_shape=(
            jax.ShapeDtypeStruct((8, 2, 32, 512), F32),
            jax.ShapeDtypeStruct((2, 2, 4, 4, 16, 256), F32),
            jax.ShapeDtypeStruct((512, 512), F32),
        ),
        in_specs=[vmem] * 2,
        out_specs=(vmem,) * 3,
        scratch_shapes=[
            *[pltpu.VMEM((512, 1024), BF16)] * 4,
            *[pltpu.VMEM((1024, 512), BF16)] * 2,
            chunks, boxes, chunks, chunks, boxes,
            *rows, pltpu.VMEM((2, 2, 4, 4, 16, 256), F32), *rows,
            *[pltpu.VMEM((2, 4, 4, 8, 256), F32)] * 2,
            pltpu.VMEM((4, 4, 8, 256), F32),
            pltpu.VMEM((3, 4, 8, 256), F32),
            pltpu.VMEM((3, 8, 256), F32),
            pltpu.VMEM((8, 8, 256), F32),
            pltpu.SemaphoreType.DMA((slots,)),
            pltpu.SemaphoreType.DMA((slots,)),
        ],
        compiler_params=pltpu.CompilerParams(
            collective_id=0, has_side_effects=True, vmem_limit_bytes=48 * 2**20
        ),
        name="power",
    )(samples, sketch)


def per_device(samples, sketch):
    y, b, inverse = power(samples, sketch)
    total_rows = samples.shape[1] * lax.axis_size("rows")
    scale = float(np.sqrt(np.float32(2 * total_rows)))
    return finish(y.reshape(512, 512), b.reshape(2, 512, 256), inverse, scale)


def solution(mesh):
    placed = (P(None, "rows", "cols"), P(None, "cols", None))
    return jax.shard_map(
        per_device,
        mesh=mesh,
        in_specs=placed,
        out_specs=(P(None, "rows", None), P(None, None, "cols")),
        check_vma=False,
    )
```

```python
import functools

import jax
import jax.numpy as jnp
import numpy as np
from jax import lax
from jax.experimental import pallas as pl
from jax.experimental.pallas import tpu as pltpu
from jax.sharding import PartitionSpec as P

MESH = pl.DeviceIdType.MESH
HI = lax.Precision.HIGHEST
F32 = jnp.float32
BF16 = jnp.bfloat16

Z_SLOTS = 56
ROW_SLOTS = 68
GRAM_SLOTS = 21


def split(value):
    high = value.astype(BF16)
    return high, (value - high.astype(F32)).astype(BF16)


class Copies:
    def __init__(self, send_sem, recv_sem):
        self.send_sem, self.recv_sem = send_sem, recv_sem
        self.made = {}

    def send(self, slot, src, dst, device):
        copy = pltpu.make_async_remote_copy(
            src_ref=src, dst_ref=dst, send_sem=self.send_sem.at[slot],
            recv_sem=self.recv_sem.at[slot], device_id=device, device_id_type=MESH,
        )
        copy.start()
        self.made[slot] = copy

    def arrived(self, slot):
        self.made[slot].wait_recv()

    def finish(self):
        for copy in self.made.values():
            copy.wait_send()


class Place:
    def __init__(self):
        self.r = lax.axis_index("rows")
        self.z = lax.axis_index("cols")
        self.core = lax.rem(self.r, 2)
        self.x = lax.rem(self.r // 2, 4)
        self.y = self.r // 8

    def along_z(self, d):
        return (self.r, lax.rem(self.z + d + 8, 8))

    def along_x(self, d):
        return ((self.y * 4 + lax.rem(self.x + d, 4)) * 2 + self.core, self.z)

    def along_y(self, d):
        return ((lax.rem(self.y + d, 4) * 4 + self.x) * 2 + self.core, self.z)

    def sibling(self):
        return (self.r + 1 - 2 * self.core, self.z)

    def line(self, axis, d):
        return self.along_x(d) if axis == 0 else self.along_y(d)

    def at(self, axis):
        return self.x if axis == 0 else self.y


def greet(place):
    barrier = pltpu.get_barrier_semaphore()
    peers = [place.sibling()]
    peers += [place.along_x(d) for d in (1, 2, 3)]
    peers += [place.along_y(d) for d in (1, 2, 3)]
    peers += [place.along_z(d) for d in range(1, 8)]
    for peer in peers:
        pl.semaphore_signal(barrier, inc=1, device_id=peer, device_id_type=MESH)
    return lambda: pl.semaphore_wait(barrier, len(peers))


def wrap8(value):
    return lax.rem(value + 16, 8)


class RingZ:
    def __init__(self, place, copies, base, part, slots, full):
        self.place, self.copies, self.base = place, copies, base
        self.part, self.slots, self.full = part, slots, full

    @staticmethod
    def box(way, quarter, dist):
        lead = (way > 0) == (quarter < 2)
        return (0 if way > 0 else 14) + (quarter % 2) * 7 + (dist - 1 if lead else 3 + dist)

    def push(self, way, quarter, dist):
        box = self.box(way, quarter, dist)
        chunk = wrap8(self.place.z + way * dist)
        self.copies.send(self.base + box, self.part.at[chunk, quarter], self.slots.at[box],
                         self.place.along_z(way))

    def pull(self, way, quarter, dist):
        box = self.box(way, quarter, dist)
        self.copies.arrived(self.base + box)
        chunk = wrap8(self.place.z + way * (dist - 1))
        self.part[chunk, quarter] = self.part[chunk, quarter] + self.slots[box]

    LEADS = ((1, 0), (-1, 2), (1, 1), (-1, 3))
    OTHERS = ((1, 2), (-1, 0), (1, 3), (-1, 1))

    def scatter_steps(self):
        for way, quarter in self.LEADS:
            self.push(way, quarter, 4)
        yield
        for way, quarter in self.OTHERS:
            self.push(way, quarter, 3)
        yield
        for step in range(3):
            for way, quarter in self.LEADS:
                self.pull(way, quarter, 4 - step)
                self.push(way, quarter, 3 - step)
            for way, quarter in self.OTHERS:
                self.pull(way, quarter, 3 - step)
                if step < 2:
                    self.push(way, quarter, 2 - step)
            yield
        for way, quarter in self.LEADS:
            self.pull(way, quarter, 1)
        yield

    def gather_steps(self):
        place, copies, full = self.place, self.copies, self.full
        full[place.z] = self.part[place.z]
        base = self.base + 28

        def slot(way, quarter, dist):
            return base + (0 if way > 0 else 14) + (quarter * 3 + dist if dist < 3 else 12 + quarter % 2)

        def push(way, quarter, dist):
            chunk = wrap8(place.z - way * dist)
            ref = full.at[chunk, quarter]
            copies.send(slot(way, quarter, dist), ref, ref, place.along_z(way))

        order = self.LEADS + self.OTHERS
        for way, quarter in order:
            push(way, quarter, 0)
        yield
        for dist in (1, 2):
            for way, quarter in order:
                copies.arrived(slot(way, quarter, dist - 1))
                push(way, quarter, dist)
            yield
        for way, quarter in self.LEADS:
            copies.arrived(slot(way, quarter, 2))
            push(way, quarter, 3)
        for way, quarter in self.OTHERS:
            copies.arrived(slot(way, quarter, 2))
        yield
        for way, quarter in self.LEADS:
            copies.arrived(slot(way, quarter, 3))
        yield


class SumRows:
    STREAMS = ((0, 0), (1, 0), (0, 1), (1, 1))

    def __init__(self, place, copies, base, part, from_core, from_line, from_point, full):
        self.place, self.copies, self.base = place, copies, base
        self.part, self.full = part, full
        self.from_core, self.from_line, self.from_point = from_core, from_line, from_point

    def slot(self, h, s, kind, d):
        return self.base + 17 * (2 * h + s) + kind + d

    def steps(self):
        place, copies, slot = self.place, self.copies, self.slot
        part, full, core = self.part, self.full, place.core
        first = [place.at(0), place.at(1)]
        second = [place.at(1), place.at(0)]
        CORE, LINE, POINT, POINT_BACK, LINE_BACK, BACK = 0, 0, 3, 6, 9, 13
        for h, s in self.STREAMS:
            copies.send(slot(h, s, CORE, 0), part.at[h, 1 - core, s], self.from_core.at[h, s], place.sibling())
        yield
        for h, s in self.STREAMS:
            copies.arrived(slot(h, s, CORE, 0))
            for d in (2, 1, 3, 0):
                at = lax.rem(first[h] + d, 4)
                part[h, core, s, at] = part[h, core, s, at] + self.from_core[h, s, at]
                if d:
                    copies.send(slot(h, s, LINE, d), part.at[h, core, s, at], self.from_line.at[h, s, d - 1],
                                place.line(h, d))
        yield
        for h, s in self.STREAMS:
            a = first[h]
            for d in (1, 2, 3):
                copies.arrived(slot(h, s, LINE, d))
            part[h, core, s, a] = (part[h, core, s, a] + self.from_line[h, s, 0]) + (
                self.from_line[h, s, 1] + self.from_line[h, s, 2])
            for d in (2, 1, 3):
                b = lax.rem(second[h] + d, 4)
                copies.send(slot(h, s, POINT, d), part.at[h, core, s, a, b], self.from_point.at[h, s, d - 1],
                            place.line(1 - h, d))
        yield
        for h, s in self.STREAMS:
            a, b = first[h], second[h]
            for d in (1, 2, 3):
                copies.arrived(slot(h, s, POINT, d))
            full[h, core, s, a, b] = (part[h, core, s, a, b] + self.from_point[h, s, 0]) + (
                self.from_point[h, s, 1] + self.from_point[h, s, 2])
            ref = full.at[h, core, s, a, b]
            for d in (2, 1, 3):
                copies.send(slot(h, s, POINT_BACK, d), ref, ref, place.line(1 - h, d))
        yield
        for h, s in self.STREAMS:
            for d in (1, 2, 3):
                copies.arrived(slot(h, s, POINT_BACK, d))
            ref = full.at[h, core, s, first[h]]
            for d in (2, 1, 3):
                copies.send(slot(h, s, LINE_BACK, d), ref, ref, place.line(h, d))
            copies.send(slot(h, s, BACK, 0), ref, ref, place.sibling())
        yield
        for h, s in self.STREAMS:
            for d in (1, 3, 2):
                copies.arrived(slot(h, s, LINE_BACK, d))
                ref = full.at[h, core, s, lax.rem(first[h] - d + 4, 4)]
                copies.send(slot(h, s, BACK, d), ref, ref, place.sibling())
        yield
        for h, s in self.STREAMS:
            for d in range(4):
                copies.arrived(slot(h, s, BACK, d))
        yield


class SumAll:
    def __init__(self, place, copies, base, part, from_core, from_line, from_point, from_z, full):
        self.place, self.copies, self.base = place, copies, base
        self.part, self.full = part, full
        self.from_core, self.from_line, self.from_point, self.from_z = (
            from_core, from_line, from_point, from_z)

    def steps(self):
        place, copies, base = self.place, self.copies, self.base
        part, full, core, x, y = self.part, self.full, place.core, place.x, place.y
        copies.send(base, part.at[1 - core], self.from_core, place.sibling())
        yield
        copies.arrived(base)
        base += 1
        part[core] = part[core] + self.from_core[...]
        for d in (2, 1, 3):
            copies.send(base + d - 1, part.at[core, lax.rem(x + d, 4)], self.from_line.at[d - 1],
                        place.along_x(d))
        yield
        for d in (1, 2, 3):
            copies.arrived(base + d - 1)
        base += 3
        part[core, x] = (part[core, x] + self.from_line[0]) + (self.from_line[1] + self.from_line[2])
        for d in (2, 1, 3):
            copies.send(base + d - 1, part.at[core, x, lax.rem(y + d, 4)], self.from_point.at[d - 1],
                        place.along_y(d))
        yield
        for d in (1, 2, 3):
            copies.arrived(base + d - 1)
        base += 3
        mine = self.from_z.at[place.z]
        mine[...] = (part[core, x, y] + self.from_point[0]) + (self.from_point[1] + self.from_point[2])
        for d in (4, 3, 5, 2, 6, 1, 7):
            copies.send(base + d - 1, mine, mine, place.along_z(d))
        yield
        for d in range(1, 8):
            copies.arrived(base + d - 1)
        base += 7
        total = self.from_z[0]
        for z in range(1, 8):
            total = total + self.from_z[z]
        full[core, x, y] = total
        ref = full.at[core, x, y]
        for d in (2, 1, 3):
            copies.send(base + d - 1, ref, ref, place.along_y(d))
        yield
        for d in (1, 2, 3):
            copies.arrived(base + d - 1)
        base += 3
        ref = full.at[core, x]
        for d in (2, 1, 3):
            copies.send(base + d - 1, ref, ref, place.along_x(d))
        yield
        for d in (1, 2, 3):
            copies.arrived(base + d - 1)
        base += 3
        ref = full.at[core]
        copies.send(base, ref, ref, place.sibling())
        yield
        copies.arrived(base)
        yield


def run(steps):
    for _ in steps:
        pass


def interleave(*many):
    live = list(many)
    while live:
        live = [one for one in live if next(one, run) is None]


def multiply(x_hi, x_lo, t_hi, t_lo, store, i):
    rows = pl.ds(pl.multiple_of(i * 256, 256), 256)
    dot = functools.partial(jnp.dot, preferred_element_type=F32)
    for j in range(2):
        lanes = pl.ds(j * 256, 256)
        xh, xl = x_hi[rows, :], x_lo[rows, :]
        th, tl = t_hi[:, lanes], t_lo[:, lanes]
        store(i, j, dot(xh, th) + (dot(xh, tl) + dot(xl, th)))


def dots(lefts, rights):
    terms = [left * right for left, right in zip(lefts, rights)]
    while len(terms) > 1:
        terms = [sum(terms[i + 1:i + 2], terms[i]) for i in range(0, len(terms), 2)]
    return terms[0]


def inverse_factor(ref, start, hook):
    groups = [ref[start + 8 * g:start + 8 * g + 8, start:start + 128] for g in range(16)]
    wide = (8, 128)
    lane = lax.broadcasted_iota(jnp.int32, wide, 1)
    sub = lax.broadcasted_iota(jnp.int32, wide, 0)

    def row(value, k):
        return jnp.broadcast_to(value[k:k + 1, :], wide)

    def col(value, k):
        return jnp.broadcast_to(value[:, k:k + 1], wide)

    for g in range(16):
        at = 8 * g
        inside = (lane >= at) & (lane < at + 8)
        own = groups[g]
        c = [col(own, at + k) for k in range(8)]
        u = jnp.where(inside, jnp.where(lane == at + sub, 1.0, 0.0), own)
        inverse = root = jnp.zeros(wide, F32)
        for k in range(8):
            pivot = row(c[k], k)
            inv = 1.0 / pivot
            inverse = jnp.where(sub == k, inv, inverse)
            root = jnp.where(sub == k, lax.rsqrt(pivot), root)
            if k < 7:
                f = jnp.where(sub > k, c[k], 0.0) * inv
                for m in range(k + 1, 8):
                    c[m] = c[m] - f * row(c[m], k)
                u = u - f * row(u, k)
        ref[start + at:start + at + 8, start:start + 128] = jnp.where(lane <= at + sub, u * root, 0.0)
        hook((start + at) // 8)
        if g == 15:
            break
        q = u * inverse
        for m in range(7, 0, -1):
            q = q - jnp.where(sub < m, c[m] * inverse, 0.0) * row(q, m)
        rows = [row(q, k) for k in range(8)]
        for v in range(g + 1, 16):
            cols = [col(groups[v], at + k) for k in range(8)]
            groups[v] = jnp.where(inside, 0.0, groups[v]) - dots(cols, rows)


def factor(m_ref, hook):
    dot = functools.partial(jnp.dot, precision=HI, preferred_element_type=F32)
    for k in range(4):
        at = 128 * k
        inverse_factor(m_ref, at, hook)
        w = m_ref[at:at + 128, at:at + 128]
        if k > 0:
            m_ref[at:at + 128, :at] = dot(w, m_ref[at:at + 128, :at])
        if k < 3:
            u = dot(w, m_ref[at:at + 128, at + 128:])
            ut = u.T
            m_ref[at + 128:, at + 128:] = m_ref[at + 128:, at + 128:] - dot(ut, u)
            if k > 0:
                m_ref[at + 128:, :at] = m_ref[at + 128:, :at] - dot(ut, m_ref[at:at + 128, :at])
            m_ref[at + 128:, at:at + 128] = -dot(ut, w)
            m_ref[at:at + 128, at + 128:] = jnp.zeros((128, 384 - at), F32)


def set_gram(packed, m_ref):
    row = lax.broadcasted_iota(jnp.int32, (256, 256), 0)
    col = lax.broadcasted_iota(jnp.int32, (256, 256), 1)
    turned = packed.T
    gram_r = jnp.where(row >= col, packed, turned)
    gram_i = jnp.where(row < col, packed, jnp.where(row > col, -turned, 0.0))
    m_ref[:256, :256] = gram_r
    m_ref[256:, 256:] = gram_r
    m_ref[256:, :256] = gram_i
    m_ref[:256, 256:] = -gram_i


def finish_kernel(scale, y_ref, b_ref, m_ref, basis_ref, proj_ref, l_hi, l_lo):
    for i in range(4):
        rows = slice(128 * i, 128 * i + 128)
        l_hi[rows, :], l_lo[rows, :] = split(m_ref[rows, :])

    def product(left_hi, left_lo, right_hi, right_lo):
        dot = functools.partial(
            lax.dot_general, dimension_numbers=(((1,), (1,)), ((), ())), preferred_element_type=F32)
        return dot(left_hi, right_hi) + (dot(left_hi, right_lo) + dot(left_lo, right_hi))

    @pl.loop(0, 2)
    def _(i):
        rows = pl.ds(i * 256, 256)
        real, imag = y_ref[rows, :256], y_ref[rows, 256:]
        basis_ref[0, rows, :] = product(*split(jnp.concatenate([real, -imag], 1)), l_hi[...], l_lo[...]) * scale
        basis_ref[1, rows, :] = product(*split(jnp.concatenate([imag, real], 1)), l_hi[...], l_lo[...]) * scale

    @pl.loop(0, 2)
    def _(i):
        rows = pl.ds(i * 256, 256)
        real, imag = b_ref[0], b_ref[1]
        hi, lo = l_hi[rows, :], l_lo[rows, :]
        proj_ref[0, rows, :] = product(hi, lo, *split(jnp.concatenate([real, -imag], 1)))
        proj_ref[1, rows, :] = product(hi, lo, *split(jnp.concatenate([imag, real], 1)))


def finish(y, b, inverse, scale):
    vmem = pl.BlockSpec(memory_space=pltpu.VMEM)
    return pl.pallas_call(
        functools.partial(finish_kernel, scale),
        out_shape=(jax.ShapeDtypeStruct((2, 512, 512), F32),) * 2,
        in_specs=[vmem] * 3,
        out_specs=(vmem,) * 2,
        scratch_shapes=[
            pltpu.VMEM((512, 512), BF16),
            pltpu.VMEM((512, 512), BF16),
        ],
        compiler_params=pltpu.CompilerParams(vmem_limit_bytes=48 * 2**20),
        name="finish",
    )(y, b, inverse)

HOOKS = (0, 8, 16, 24, 32, 42, 50)


def power_kernel(a_hbm, s_hbm, y_ref, b_ref, m_ref, x_hi, x_lo, xt_hi, xt_lo, t_hi, t_lo,
                 z_part, z_slots, z_full, z_part2, z_slots2,
                 r_part, r_core, r_line, r_point, r_full, r_part2, r_core2, r_line2, r_point2,
                 g_ref, g_part, g_core, g_line, g_point, g_z, a_ref, s_ref, in_sem, send_sem, recv_sem):
    place = Place()
    all_here = greet(place)
    copies = Copies(send_sem, recv_sem)

    def set_pair(rows, real, imag, sign):
        low = pl.ds(rows, real.shape[0])
        high = pl.ds(512 + rows, real.shape[0])
        for at, lanes, value in (
            (low, slice(0, 256), real), (low, slice(256, 512), imag),
            (high, slice(0, 256), sign * imag), (high, slice(256, 512), -sign * real),
        ):
            t_hi[at, lanes], t_lo[at, lanes] = split(value)

    fetches = [
        pltpu.make_async_copy(src, dst, in_sem.at[n])
        for n, (src, dst) in enumerate(((s_hbm, s_ref), (a_hbm, a_ref)))
    ]
    for fetch in fetches:
        fetch.start()
    fetches[0].wait()

    @pl.loop(0, 8)
    def _(i):
        rows = pl.ds(i * 64, 64)
        set_pair(i * 64, s_ref[0, rows, :], s_ref[1, rows, :], -1.0)

    fetches[1].wait()

    @pl.loop(0, 8)
    def _(i):
        rows = pl.ds(i * 64, 64)
        for p in (0, 1):
            x_hi[rows, p * 512:(p + 1) * 512], x_lo[rows, p * 512:(p + 1) * 512] = split(a_ref[p, rows, :])

    def store_chunks(ref):
        def store(i, j, tile):
            ref[pl.ds(i * 4, 4), :, :, j * 256:(j + 1) * 256] = tile.reshape(4, 4, 16, 256)
        return store

    def store_rows(ref):
        def store(i, j, tile):
            ref[j, i] = tile.reshape(2, 4, 4, 8, 256)
        return store

    far = 1 - place.z // 4
    ring = RingZ(place, copies, 0, z_part, z_slots, z_full)
    steps = ring.scatter_steps()
    multiply(x_hi, x_lo, t_hi, t_lo, store_chunks(z_part), far)
    all_here()
    next(steps)
    multiply(x_hi, x_lo, t_hi, t_lo, store_chunks(z_part), 1 - far)
    next(steps)

    @pl.loop(0, 4)
    def _(i):
        for p in (0, 1):
            rows = pl.ds(i * 128, 128)
            block = a_ref[p, :, rows].T
            lanes = slice(p * 512, (p + 1) * 512)
            xt_hi[rows, lanes], xt_lo[rows, lanes] = split(block)

    run(steps)
    run(ring.gather_steps())

    def chunks_to_t(ref):
        @pl.loop(0, 8)
        def _(i):
            value = ref[i].reshape(64, 512)
            set_pair(i * 64, value[:, :256], value[:, 256:], 1.0)

    chunks_to_t(z_full)
    multiply(xt_hi, xt_lo, t_hi, t_lo, store_rows(r_part), 1 - place.core)
    steps = SumRows(place, copies, Z_SLOTS, r_part, r_core, r_line, r_point, r_full).steps()
    next(steps)
    multiply(xt_hi, xt_lo, t_hi, t_lo, store_rows(r_part), place.core)
    run(steps)

    for k in (0, 1):
        for s in (0, 1):
            @pl.loop(0, 2)
            def _(i):
                at, lines = k * 256 + s * 128 + i * 64, pl.ds(i * 2, 2)
                set_pair(at, r_full[0, k, s, lines].reshape(64, 256), r_full[1, k, s, lines].reshape(64, 256), -1.0)

    ring = RingZ(place, copies, Z_SLOTS + ROW_SLOTS, z_part2, z_slots2, y_ref)
    steps = ring.scatter_steps()
    multiply(x_hi, x_lo, t_hi, t_lo, store_chunks(z_part2), far)
    next(steps)
    multiply(x_hi, x_lo, t_hi, t_lo, store_chunks(z_part2), 1 - far)
    run(steps)
    mine = z_part2[place.z].reshape(64, 512)
    steps = ring.gather_steps()
    next(steps)
    real, imag = mine[:, :256], mine[:, 256:]
    tall = jnp.concatenate([real, imag], 0).T
    gram_r = jnp.dot(tall, jnp.concatenate([real, imag], 0), precision=HI, preferred_element_type=F32)
    gram_i = jnp.dot(tall, jnp.concatenate([imag, -real], 0), precision=HI, preferred_element_type=F32)
    low = lax.broadcasted_iota(jnp.int32, (256, 256), 0) >= lax.broadcasted_iota(jnp.int32, (256, 256), 1)
    g_part[...] = jnp.where(low, gram_r, gram_i).reshape(2, 4, 4, 8, 256)
    gram_steps = SumAll(place, copies, 2 * Z_SLOTS + ROW_SLOTS, g_part, g_core, g_line, g_point, g_z, g_ref).steps()
    for _ in range(4):
        next(gram_steps)
    next(steps)
    next(gram_steps)
    next(steps)
    next(gram_steps)
    next(steps)
    run(gram_steps)

    def behind():
        run(steps)
        chunks_to_t(y_ref)
        multiply(xt_hi, xt_lo, t_hi, t_lo, store_rows(r_part2), 1 - place.core)
        tail = SumRows(place, copies, 2 * Z_SLOTS + ROW_SLOTS + GRAM_SLOTS, r_part2, r_core2, r_line2,
                       r_point2, b_ref).steps()
        next(tail)
        multiply(xt_hi, xt_lo, t_hi, t_lo, store_rows(r_part2), place.core)
        yield
        yield from tail

    rest = behind()

    def hook(done):
        if done in HOOKS:
            next(rest)

    set_gram(g_ref[...].reshape(256, 256), m_ref)
    factor(m_ref, hook)
    run(rest)
    copies.finish()


def power(samples, sketch):
    vmem = pl.BlockSpec(memory_space=pltpu.VMEM)
    slots = 2 * Z_SLOTS + 2 * ROW_SLOTS + GRAM_SLOTS
    chunks = pltpu.VMEM((8, 4, 16, 512), F32)
    boxes = pltpu.VMEM((28, 16, 512), F32)
    rows = [
        pltpu.VMEM((2, 2, 2, 4, 4, 8, 256), F32),
        pltpu.VMEM((2, 2, 4, 4, 8, 256), F32),
        pltpu.VMEM((2, 2, 3, 4, 8, 256), F32),
        pltpu.VMEM((2, 2, 3, 8, 256), F32),
    ]
    return pl.pallas_call(
        power_kernel,
        out_shape=(
            jax.ShapeDtypeStruct((8, 4, 16, 512), F32),
            jax.ShapeDtypeStruct((2, 2, 2, 4, 4, 8, 256), F32),
            jax.ShapeDtypeStruct((512, 512), F32),
        ),
        in_specs=[pl.BlockSpec(memory_space=pl.ANY)] * 2,
        out_specs=(vmem,) * 3,
        scratch_shapes=[
            *[pltpu.VMEM((512, 1024), BF16)] * 4,
            *[pltpu.VMEM((1024, 512), BF16)] * 2,
            chunks, boxes, chunks, chunks, boxes,
            *rows, pltpu.VMEM((2, 2, 2, 4, 4, 8, 256), F32), *rows,
            *[pltpu.VMEM((2, 4, 4, 8, 256), F32)] * 2,
            pltpu.VMEM((4, 4, 8, 256), F32),
            pltpu.VMEM((3, 4, 8, 256), F32),
            pltpu.VMEM((3, 8, 256), F32),
            pltpu.VMEM((8, 8, 256), F32),
            pltpu.VMEM((2, 512, 512), F32),
            pltpu.VMEM((2, 512, 256), F32),
            pltpu.SemaphoreType.DMA((2,)),
            *[pltpu.SemaphoreType.DMA((slots,))] * 2,
        ],
        compiler_params=pltpu.CompilerParams(
            collective_id=0, has_side_effects=True, vmem_limit_bytes=50 * 2**20
        ),
        name="power",
    )(samples, sketch)


def per_device(samples, sketch):
    y, b, inverse = power(samples, sketch)
    total_rows = samples.shape[1] * lax.axis_size("rows")
    scale = float(np.sqrt(np.float32(2 * total_rows)))
    return finish(y.reshape(512, 512), b.reshape(2, 512, 256), inverse, scale)


def solution(mesh):
    placed = (P(None, "rows", "cols"), P(None, "cols", None))
    return jax.shard_map(
        per_device,
        mesh=mesh,
        in_specs=placed,
        out_specs=(P(None, "rows", None), P(None, None, "cols")),
        check_vma=False,
    )
```

```python
import functools

import jax
import jax.numpy as jnp
import numpy as np
from jax import lax
from jax.experimental import pallas as pl
from jax.experimental.pallas import tpu as pltpu
from jax.sharding import PartitionSpec as P

MESH = pl.DeviceIdType.MESH
HI = lax.Precision.HIGHEST
F32 = jnp.float32
BF16 = jnp.bfloat16

Z_SLOTS = 56
ROW_SLOTS = 68
GRAM_SLOTS = 21


def split(value):
    high = value.astype(BF16)
    return high, (value - high.astype(F32)).astype(BF16)


class Copies:
    def __init__(self, send_sem, recv_sem):
        self.send_sem, self.recv_sem = send_sem, recv_sem
        self.made = {}

    def send(self, slot, src, dst, device):
        copy = pltpu.make_async_remote_copy(
            src_ref=src, dst_ref=dst, send_sem=self.send_sem.at[slot],
            recv_sem=self.recv_sem.at[slot], device_id=device, device_id_type=MESH,
        )
        copy.start()
        self.made[slot] = copy

    def arrived(self, slot):
        self.made[slot].wait_recv()

    def finish(self):
        for copy in self.made.values():
            copy.wait_send()


class Place:
    def __init__(self):
        self.r = lax.axis_index("rows")
        self.z = lax.axis_index("cols")
        self.core = lax.rem(self.r, 2)
        self.x = lax.rem(self.r // 2, 4)
        self.y = self.r // 8

    def along_z(self, d):
        return (self.r, lax.rem(self.z + d + 8, 8))

    def along_x(self, d):
        return ((self.y * 4 + lax.rem(self.x + d, 4)) * 2 + self.core, self.z)

    def along_y(self, d):
        return ((lax.rem(self.y + d, 4) * 4 + self.x) * 2 + self.core, self.z)

    def sibling(self):
        return (self.r + 1 - 2 * self.core, self.z)

    def line(self, axis, d):
        return self.along_x(d) if axis == 0 else self.along_y(d)

    def at(self, axis):
        return self.x if axis == 0 else self.y


def greet(place):
    barrier = pltpu.get_barrier_semaphore()
    peers = [place.sibling()]
    peers += [place.along_x(d) for d in (1, 2, 3)]
    peers += [place.along_y(d) for d in (1, 2, 3)]
    peers += [place.along_z(d) for d in range(1, 8)]
    for peer in peers:
        pl.semaphore_signal(barrier, inc=1, device_id=peer, device_id_type=MESH)
    return lambda: pl.semaphore_wait(barrier, len(peers))


def wrap8(value):
    return lax.rem(value + 16, 8)


class RingZ:
    def __init__(self, place, copies, base, part, slots, full):
        self.place, self.copies, self.base = place, copies, base
        self.part, self.slots, self.full = part, slots, full

    @staticmethod
    def box(way, quarter, dist):
        lead = (way > 0) == (quarter < 2)
        return (0 if way > 0 else 14) + (quarter % 2) * 7 + (dist - 1 if lead else 3 + dist)

    def push(self, way, quarter, dist):
        box = self.box(way, quarter, dist)
        chunk = wrap8(self.place.z + way * dist)
        self.copies.send(self.base + box, self.part.at[chunk, quarter], self.slots.at[box],
                         self.place.along_z(way))

    def pull(self, way, quarter, dist):
        box = self.box(way, quarter, dist)
        self.copies.arrived(self.base + box)
        chunk = wrap8(self.place.z + way * (dist - 1))
        self.part[chunk, quarter] = self.part[chunk, quarter] + self.slots[box]

    LEADS = ((1, 0), (-1, 2), (1, 1), (-1, 3))
    OTHERS = ((1, 2), (-1, 0), (1, 3), (-1, 1))

    def scatter_steps(self):
        for way, quarter in self.LEADS:
            self.push(way, quarter, 4)
        yield
        for way, quarter in self.OTHERS:
            self.push(way, quarter, 3)
        yield
        for step in range(3):
            for way, quarter in self.LEADS:
                self.pull(way, quarter, 4 - step)
                self.push(way, quarter, 3 - step)
            for way, quarter in self.OTHERS:
                self.pull(way, quarter, 3 - step)
                if step < 2:
                    self.push(way, quarter, 2 - step)
            yield
        z = self.place.z
        for way, quarter in self.LEADS:
            self.pull(way, quarter, 1)
            self.full[z, quarter] = self.part[z, quarter]
            for to in (1, -1):
                self.push_on(to, quarter, 0)
        yield

    def gather_slot(self, way, quarter, dist):
        return self.base + 28 + (0 if way > 0 else 14) + (quarter * 3 + dist if dist < 3 else 12 + quarter % 2)

    def push_on(self, way, quarter, dist):
        ref = self.full.at[wrap8(self.place.z - way * dist), quarter]
        self.copies.send(self.gather_slot(way, quarter, dist), ref, ref, self.place.along_z(way))

    def gather_steps(self):
        copies, slot, push = self.copies, self.gather_slot, self.push_on
        order = self.LEADS + self.OTHERS
        for dist in (1, 2):
            for way, quarter in order:
                copies.arrived(slot(way, quarter, dist - 1))
                push(way, quarter, dist)
            yield
        for way, quarter in self.LEADS:
            copies.arrived(slot(way, quarter, 2))
            push(way, quarter, 3)
        for way, quarter in self.OTHERS:
            copies.arrived(slot(way, quarter, 2))
        yield
        for way, quarter in self.LEADS:
            copies.arrived(slot(way, quarter, 3))
        yield


class SumRows:
    STREAMS = ((0, 0), (1, 0), (0, 1), (1, 1))

    def __init__(self, place, copies, base, part, from_core, from_line, from_point, full):
        self.place, self.copies, self.base = place, copies, base
        self.part, self.full = part, full
        self.from_core, self.from_line, self.from_point = from_core, from_line, from_point

    def slot(self, h, s, kind, d):
        return self.base + 17 * (2 * h + s) + kind + d

    def steps(self):
        place, copies, slot = self.place, self.copies, self.slot
        part, full, core = self.part, self.full, place.core
        first = [place.at(0), place.at(1)]
        second = [place.at(1), place.at(0)]
        CORE, LINE, POINT, POINT_BACK, LINE_BACK, BACK = 0, 0, 3, 6, 9, 13
        for h, s in self.STREAMS:
            copies.send(slot(h, s, CORE, 0), part.at[h, 1 - core, s], self.from_core.at[h, s], place.sibling())
        yield
        for h, s in self.STREAMS:
            copies.arrived(slot(h, s, CORE, 0))
            for d in (2, 1, 3, 0):
                at = lax.rem(first[h] + d, 4)
                part[h, core, s, at] = part[h, core, s, at] + self.from_core[h, s, at]
                if d:
                    copies.send(slot(h, s, LINE, d), part.at[h, core, s, at], self.from_line.at[h, s, d - 1],
                                place.line(h, d))
        yield
        for h, s in self.STREAMS:
            a = first[h]
            for d in (1, 2, 3):
                copies.arrived(slot(h, s, LINE, d))
            part[h, core, s, a] = (part[h, core, s, a] + self.from_line[h, s, 0]) + (
                self.from_line[h, s, 1] + self.from_line[h, s, 2])
            for d in (2, 1, 3):
                b = lax.rem(second[h] + d, 4)
                copies.send(slot(h, s, POINT, d), part.at[h, core, s, a, b], self.from_point.at[h, s, d - 1],
                            place.line(1 - h, d))
        yield
        for h, s in self.STREAMS:
            a, b = first[h], second[h]
            for d in (1, 2, 3):
                copies.arrived(slot(h, s, POINT, d))
            full[h, core, s, a, b] = (part[h, core, s, a, b] + self.from_point[h, s, 0]) + (
                self.from_point[h, s, 1] + self.from_point[h, s, 2])
            ref = full.at[h, core, s, a, b]
            for d in (2, 1, 3):
                copies.send(slot(h, s, POINT_BACK, d), ref, ref, place.line(1 - h, d))
        yield
        for h, s in self.STREAMS:
            for d in (1, 2, 3):
                copies.arrived(slot(h, s, POINT_BACK, d))
            ref = full.at[h, core, s, first[h]]
            for d in (2, 1, 3):
                copies.send(slot(h, s, LINE_BACK, d), ref, ref, place.line(h, d))
            copies.send(slot(h, s, BACK, 0), ref, ref, place.sibling())
        yield
        for h, s in self.STREAMS:
            for d in (1, 3, 2):
                copies.arrived(slot(h, s, LINE_BACK, d))
                ref = full.at[h, core, s, lax.rem(first[h] - d + 4, 4)]
                copies.send(slot(h, s, BACK, d), ref, ref, place.sibling())
        yield
        for h, s in self.STREAMS:
            for d in range(4):
                copies.arrived(slot(h, s, BACK, d))
        yield


class SumAll:
    def __init__(self, place, copies, base, part, from_core, from_line, from_point, from_z, full):
        self.place, self.copies, self.base = place, copies, base
        self.part, self.full = part, full
        self.from_core, self.from_line, self.from_point, self.from_z = (
            from_core, from_line, from_point, from_z)

    def steps(self):
        place, copies, base = self.place, self.copies, self.base
        part, full, core, x, y = self.part, self.full, place.core, place.x, place.y
        copies.send(base, part.at[1 - core], self.from_core, place.sibling())
        yield
        copies.arrived(base)
        base += 1
        part[core] = part[core] + self.from_core[...]
        for d in (2, 1, 3):
            copies.send(base + d - 1, part.at[core, lax.rem(x + d, 4)], self.from_line.at[d - 1],
                        place.along_x(d))
        yield
        for d in (1, 2, 3):
            copies.arrived(base + d - 1)
        base += 3
        part[core, x] = (part[core, x] + self.from_line[0]) + (self.from_line[1] + self.from_line[2])
        for d in (2, 1, 3):
            copies.send(base + d - 1, part.at[core, x, lax.rem(y + d, 4)], self.from_point.at[d - 1],
                        place.along_y(d))
        yield
        for d in (1, 2, 3):
            copies.arrived(base + d - 1)
        base += 3
        mine = self.from_z.at[place.z]
        mine[...] = (part[core, x, y] + self.from_point[0]) + (self.from_point[1] + self.from_point[2])
        for d in (4, 3, 5, 2, 6, 1, 7):
            copies.send(base + d - 1, mine, mine, place.along_z(d))
        yield
        for d in range(1, 8):
            copies.arrived(base + d - 1)
        base += 7
        total = self.from_z[0]
        for z in range(1, 8):
            total = total + self.from_z[z]
        full[core, x, y] = total
        ref = full.at[core, x, y]
        for d in (2, 1, 3):
            copies.send(base + d - 1, ref, ref, place.along_y(d))
        yield
        for d in (1, 2, 3):
            copies.arrived(base + d - 1)
        base += 3
        ref = full.at[core, x]
        for d in (2, 1, 3):
            copies.send(base + d - 1, ref, ref, place.along_x(d))
        yield
        for d in (1, 2, 3):
            copies.arrived(base + d - 1)
        base += 3
        ref = full.at[core]
        copies.send(base, ref, ref, place.sibling())
        yield
        copies.arrived(base)
        yield


def run(steps):
    for _ in steps:
        pass


def interleave(*many):
    live = list(many)
    while live:
        live = [one for one in live if next(one, run) is None]


def multiply(x_hi, x_lo, t_hi, t_lo, store, i):
    rows = pl.ds(pl.multiple_of(i * 256, 256), 256)
    dot = functools.partial(jnp.dot, preferred_element_type=F32)
    for j in range(2):
        lanes = pl.ds(j * 256, 256)
        xh, xl = x_hi[rows, :], x_lo[rows, :]
        th, tl = t_hi[:, lanes], t_lo[:, lanes]
        store(i, j, dot(xh, th) + (dot(xh, tl) + dot(xl, th)))


def dots(lefts, rights):
    terms = [left * right for left, right in zip(lefts, rights)]
    while len(terms) > 1:
        terms = [sum(terms[i + 1:i + 2], terms[i]) for i in range(0, len(terms), 2)]
    return terms[0]


def inverse_factor(ref, start, hook):
    groups = [ref[start + 8 * g:start + 8 * g + 8, start:start + 128] for g in range(16)]
    wide = (8, 128)
    lane = lax.broadcasted_iota(jnp.int32, wide, 1)
    sub = lax.broadcasted_iota(jnp.int32, wide, 0)

    def row(value, k):
        return jnp.broadcast_to(value[k:k + 1, :], wide)

    def col(value, k):
        return jnp.broadcast_to(value[:, k:k + 1], wide)

    for g in range(16):
        at = 8 * g
        inside = (lane >= at) & (lane < at + 8)
        own = groups[g]
        c = [col(own, at + k) for k in range(8)]
        u = jnp.where(inside, jnp.where(lane == at + sub, 1.0, 0.0), own)
        inverse = root = jnp.zeros(wide, F32)
        for k in range(8):
            pivot = row(c[k], k)
            inv = 1.0 / pivot
            inverse = jnp.where(sub == k, inv, inverse)
            root = jnp.where(sub == k, lax.rsqrt(pivot), root)
            if k < 7:
                f = jnp.where(sub > k, c[k], 0.0) * inv
                for m in range(k + 1, 8):
                    c[m] = c[m] - f * row(c[m], k)
                u = u - f * row(u, k)
        ref[start + at:start + at + 8, start:start + 128] = jnp.where(lane <= at + sub, u * root, 0.0)
        hook((start + at) // 8)
        if g == 15:
            break
        q = u * inverse
        for m in range(7, 0, -1):
            q = q - jnp.where(sub < m, c[m] * inverse, 0.0) * row(q, m)
        rows = [row(q, k) for k in range(8)]
        near = min(g + 3, 16)
        if near < 16:
            below = jnp.concatenate(groups[near:], 0)
            zeros = [jnp.zeros((at, 128), F32)] if g else []
            step = jnp.concatenate(zeros + [q, jnp.zeros((120 - at, 128), F32)], 0)
            change = jnp.dot(below, step, precision=HI, preferred_element_type=F32)
        for v in range(g + 1, near):
            cols = [col(groups[v], at + k) for k in range(8)]
            groups[v] = jnp.where(inside, 0.0, groups[v]) - dots(cols, rows)
        for v in range(near, 16):
            groups[v] = jnp.where(inside, 0.0, groups[v]) - change[8 * (v - near):8 * (v - near) + 8]


def factor(m_ref, hook):
    dot = functools.partial(jnp.dot, precision=HI, preferred_element_type=F32)
    for k in range(4):
        at = 128 * k
        inverse_factor(m_ref, at, hook)
        w = m_ref[at:at + 128, at:at + 128]
        if k > 0:
            m_ref[at:at + 128, :at] = dot(w, m_ref[at:at + 128, :at])
        if k < 3:
            u = dot(w, m_ref[at:at + 128, at + 128:])
            ut = u.T
            m_ref[at + 128:, at + 128:] = m_ref[at + 128:, at + 128:] - dot(ut, u)
            if k > 0:
                m_ref[at + 128:, :at] = m_ref[at + 128:, :at] - dot(ut, m_ref[at:at + 128, :at])
            m_ref[at + 128:, at:at + 128] = -dot(ut, w)
            m_ref[at:at + 128, at + 128:] = jnp.zeros((128, 384 - at), F32)


def set_gram(packed, m_ref):
    row = lax.broadcasted_iota(jnp.int32, (256, 256), 0)
    col = lax.broadcasted_iota(jnp.int32, (256, 256), 1)
    turned = packed.T
    gram_r = jnp.where(row >= col, packed, turned)
    gram_i = jnp.where(row < col, packed, jnp.where(row > col, -turned, 0.0))
    m_ref[:256, :256] = gram_r
    m_ref[256:, 256:] = gram_r
    m_ref[256:, :256] = gram_i
    m_ref[:256, 256:] = -gram_i


def finish_kernel(scale, y_ref, b_ref, m_ref, basis_ref, proj_ref, l_hi, l_lo):
    for i in range(4):
        rows = slice(128 * i, 128 * i + 128)
        l_hi[rows, :], l_lo[rows, :] = split(m_ref[rows, :])

    def product(left_hi, left_lo, right_hi, right_lo):
        dot = functools.partial(
            lax.dot_general, dimension_numbers=(((1,), (1,)), ((), ())), preferred_element_type=F32)
        return dot(left_hi, right_hi) + (dot(left_hi, right_lo) + dot(left_lo, right_hi))

    @pl.loop(0, 2)
    def _(i):
        rows = pl.ds(i * 256, 256)
        real, imag = y_ref[rows, :256], y_ref[rows, 256:]
        basis_ref[0, rows, :] = product(*split(jnp.concatenate([real, -imag], 1)), l_hi[...], l_lo[...]) * scale
        basis_ref[1, rows, :] = product(*split(jnp.concatenate([imag, real], 1)), l_hi[...], l_lo[...]) * scale

    @pl.loop(0, 2)
    def _(i):
        rows = pl.ds(i * 256, 256)
        real, imag = b_ref[0], b_ref[1]
        hi, lo = l_hi[rows, :], l_lo[rows, :]
        proj_ref[0, rows, :] = product(hi, lo, *split(jnp.concatenate([real, -imag], 1)))
        proj_ref[1, rows, :] = product(hi, lo, *split(jnp.concatenate([imag, real], 1)))


def finish(y, b, inverse, scale):
    vmem = pl.BlockSpec(memory_space=pltpu.VMEM)
    return pl.pallas_call(
        functools.partial(finish_kernel, scale),
        out_shape=(jax.ShapeDtypeStruct((2, 512, 512), F32),) * 2,
        in_specs=[vmem] * 3,
        out_specs=(vmem,) * 2,
        scratch_shapes=[
            pltpu.VMEM((512, 512), BF16),
            pltpu.VMEM((512, 512), BF16),
        ],
        compiler_params=pltpu.CompilerParams(vmem_limit_bytes=48 * 2**20),
        name="finish",
    )(y, b, inverse)

ORDER = "ggygygygybgtgg"
HOOKS = (3, 14, 25, 38, 48)


def power_kernel(a_hbm, s_hbm, y_ref, b_ref, m_ref, x_hi, x_lo, xt_hi, xt_lo, t_hi, t_lo,
                 z_part, z_slots, z_full, z_part2, z_slots2,
                 r_part, r_core, r_line, r_point, r_full, r_part2, r_core2, r_line2, r_point2,
                 g_ref, g_part, g_core, g_line, g_point, g_z, a_ref, s_ref, in_sem, send_sem, recv_sem):
    place = Place()
    all_here = greet(place)
    copies = Copies(send_sem, recv_sem)

    def set_pair(rows, real, imag, sign):
        low = pl.ds(rows, real.shape[0])
        high = pl.ds(512 + rows, real.shape[0])
        for at, lanes, value in (
            (low, slice(0, 256), real), (low, slice(256, 512), imag),
            (high, slice(0, 256), sign * imag), (high, slice(256, 512), -sign * real),
        ):
            t_hi[at, lanes], t_lo[at, lanes] = split(value)

    fetches = [
        pltpu.make_async_copy(src, dst, in_sem.at[n])
        for n, (src, dst) in enumerate(((s_hbm, s_ref), (a_hbm, a_ref)))
    ]
    for fetch in fetches:
        fetch.start()
    fetches[0].wait()

    @pl.loop(0, 8)
    def _(i):
        rows = pl.ds(i * 64, 64)
        set_pair(i * 64, s_ref[0, rows, :], s_ref[1, rows, :], -1.0)

    fetches[1].wait()

    @pl.loop(0, 8)
    def _(i):
        rows = pl.ds(i * 64, 64)
        for p in (0, 1):
            x_hi[rows, p * 512:(p + 1) * 512], x_lo[rows, p * 512:(p + 1) * 512] = split(a_ref[p, rows, :])

    def store_chunks(ref):
        def store(i, j, tile):
            ref[pl.ds(i * 4, 4), :, :, j * 256:(j + 1) * 256] = tile.reshape(4, 4, 16, 256)
        return store

    def store_rows(ref):
        def store(i, j, tile):
            ref[j, i] = tile.reshape(2, 4, 4, 8, 256)
        return store

    far = 1 - place.z // 4
    ring = RingZ(place, copies, 0, z_part, z_slots, z_full)
    steps = ring.scatter_steps()
    multiply(x_hi, x_lo, t_hi, t_lo, store_chunks(z_part), far)
    all_here()
    next(steps)
    multiply(x_hi, x_lo, t_hi, t_lo, store_chunks(z_part), 1 - far)
    next(steps)

    @pl.loop(0, 4)
    def _(i):
        for p in (0, 1):
            rows = pl.ds(i * 128, 128)
            block = a_ref[p, :, rows].T
            lanes = slice(p * 512, (p + 1) * 512)
            xt_hi[rows, lanes], xt_lo[rows, lanes] = split(block)

    run(steps)
    run(ring.gather_steps())

    def chunks_to_t(ref):
        @pl.loop(0, 8)
        def _(i):
            value = ref[i].reshape(64, 512)
            set_pair(i * 64, value[:, :256], value[:, 256:], 1.0)

    chunks_to_t(z_full)
    multiply(xt_hi, xt_lo, t_hi, t_lo, store_rows(r_part), 1 - place.core)
    steps = SumRows(place, copies, Z_SLOTS, r_part, r_core, r_line, r_point, r_full).steps()
    next(steps)
    multiply(xt_hi, xt_lo, t_hi, t_lo, store_rows(r_part), place.core)
    run(steps)

    for k in (0, 1):
        for s in (0, 1):
            @pl.loop(0, 2)
            def _(i):
                at, lines = k * 256 + s * 128 + i * 64, pl.ds(i * 2, 2)
                set_pair(at, r_full[0, k, s, lines].reshape(64, 256), r_full[1, k, s, lines].reshape(64, 256), -1.0)

    ring = RingZ(place, copies, Z_SLOTS + ROW_SLOTS, z_part2, z_slots2, y_ref)
    steps = ring.scatter_steps()
    multiply(x_hi, x_lo, t_hi, t_lo, store_chunks(z_part2), far)
    next(steps)
    multiply(x_hi, x_lo, t_hi, t_lo, store_chunks(z_part2), 1 - far)
    run(steps)
    mine = z_part2[place.z].reshape(64, 512)
    steps = ring.gather_steps()
    real, imag = mine[:, :256], mine[:, 256:]
    tall = jnp.concatenate([real, imag], 0).T
    gram_r = jnp.dot(tall, jnp.concatenate([real, imag], 0), precision=HI, preferred_element_type=F32)
    gram_i = jnp.dot(tall, jnp.concatenate([imag, -real], 0), precision=HI, preferred_element_type=F32)
    low = lax.broadcasted_iota(jnp.int32, (256, 256), 0) >= lax.broadcasted_iota(jnp.int32, (256, 256), 1)
    g_part[...] = jnp.where(low, gram_r, gram_i).reshape(2, 4, 4, 8, 256)
    gram_steps = SumAll(place, copies, 2 * Z_SLOTS + ROW_SLOTS, g_part, g_core, g_line, g_point, g_z, g_ref).steps()
    tail = SumRows(place, copies, 2 * Z_SLOTS + ROW_SLOTS + GRAM_SLOTS, r_part2, r_core2, r_line2,
                   r_point2, b_ref).steps()

    def start_b():
        chunks_to_t(y_ref)
        multiply(xt_hi, xt_lo, t_hi, t_lo, store_rows(r_part2), 1 - place.core)
        next(tail)
        multiply(xt_hi, xt_lo, t_hi, t_lo, store_rows(r_part2), place.core)

    for turn in ORDER:
        if turn == "g":
            next(gram_steps)
        elif turn == "y":
            next(steps)
        elif turn == "b":
            start_b()
        else:
            next(tail)

    def hook(done):
        if done in HOOKS:
            next(tail)

    set_gram(g_ref[...].reshape(256, 256), m_ref)
    factor(m_ref, hook)
    run(tail)
    copies.finish()


def power(samples, sketch):
    vmem = pl.BlockSpec(memory_space=pltpu.VMEM)
    slots = 2 * Z_SLOTS + 2 * ROW_SLOTS + GRAM_SLOTS
    chunks = pltpu.VMEM((8, 4, 16, 512), F32)
    boxes = pltpu.VMEM((28, 16, 512), F32)
    rows = [
        pltpu.VMEM((2, 2, 2, 4, 4, 8, 256), F32),
        pltpu.VMEM((2, 2, 4, 4, 8, 256), F32),
        pltpu.VMEM((2, 2, 3, 4, 8, 256), F32),
        pltpu.VMEM((2, 2, 3, 8, 256), F32),
    ]
    return pl.pallas_call(
        power_kernel,
        out_shape=(
            jax.ShapeDtypeStruct((8, 4, 16, 512), F32),
            jax.ShapeDtypeStruct((2, 2, 2, 4, 4, 8, 256), F32),
            jax.ShapeDtypeStruct((512, 512), F32),
        ),
        in_specs=[pl.BlockSpec(memory_space=pl.ANY)] * 2,
        out_specs=(vmem,) * 3,
        scratch_shapes=[
            *[pltpu.VMEM((512, 1024), BF16)] * 4,
            *[pltpu.VMEM((1024, 512), BF16)] * 2,
            chunks, boxes, chunks, chunks, boxes,
            *rows, pltpu.VMEM((2, 2, 2, 4, 4, 8, 256), F32), *rows,
            *[pltpu.VMEM((2, 4, 4, 8, 256), F32)] * 2,
            pltpu.VMEM((4, 4, 8, 256), F32),
            pltpu.VMEM((3, 4, 8, 256), F32),
            pltpu.VMEM((3, 8, 256), F32),
            pltpu.VMEM((8, 8, 256), F32),
            pltpu.VMEM((2, 512, 512), F32),
            pltpu.VMEM((2, 512, 256), F32),
            pltpu.SemaphoreType.DMA((2,)),
            *[pltpu.SemaphoreType.DMA((slots,))] * 2,
        ],
        compiler_params=pltpu.CompilerParams(
            collective_id=0, has_side_effects=True, vmem_limit_bytes=50 * 2**20
        ),
        name="power",
    )(samples, sketch)


def per_device(samples, sketch):
    y, b, inverse = power(samples, sketch)
    total_rows = samples.shape[1] * lax.axis_size("rows")
    scale = float(np.sqrt(np.float32(2 * total_rows)))
    return finish(y.reshape(512, 512), b.reshape(2, 512, 256), inverse, scale)


def solution(mesh):
    placed = (P(None, "rows", "cols"), P(None, "cols", None))
    return jax.shard_map(
        per_device,
        mesh=mesh,
        in_specs=placed,
        out_specs=(P(None, "rows", None), P(None, None, "cols")),
        check_vma=False,
    )
```

```python
import functools

import jax
import jax.numpy as jnp
import numpy as np
from jax import lax
from jax.experimental import pallas as pl
from jax.experimental.pallas import tpu as pltpu
from jax.sharding import PartitionSpec as P

MESH = pl.DeviceIdType.MESH
HI = lax.Precision.HIGHEST
F32 = jnp.float32
BF16 = jnp.bfloat16

Z_SLOTS = 56
ROW_SLOTS = 68
GRAM_SLOTS = 21


def split(value):
    high = value.astype(BF16)
    return high, (value - high.astype(F32)).astype(BF16)


class Copies:
    def __init__(self, send_sem, recv_sem):
        self.send_sem, self.recv_sem = send_sem, recv_sem
        self.made = {}

    def send(self, slot, src, dst, device):
        copy = pltpu.make_async_remote_copy(
            src_ref=src, dst_ref=dst, send_sem=self.send_sem.at[slot],
            recv_sem=self.recv_sem.at[slot], device_id=device, device_id_type=MESH,
        )
        copy.start()
        self.made[slot] = copy

    def arrived(self, slot):
        self.made[slot].wait_recv()

    def finish(self):
        for copy in self.made.values():
            copy.wait_send()


class Place:
    def __init__(self):
        self.r = lax.axis_index("rows")
        self.z = lax.axis_index("cols")
        self.core = lax.rem(self.r, 2)
        self.x = lax.rem(self.r // 2, 4)
        self.y = self.r // 8

    def along_z(self, d):
        return (self.r, lax.rem(self.z + d + 8, 8))

    def along_x(self, d):
        return ((self.y * 4 + lax.rem(self.x + d, 4)) * 2 + self.core, self.z)

    def along_y(self, d):
        return ((lax.rem(self.y + d, 4) * 4 + self.x) * 2 + self.core, self.z)

    def sibling(self):
        return (self.r + 1 - 2 * self.core, self.z)

    def line(self, axis, d):
        return self.along_x(d) if axis == 0 else self.along_y(d)

    def at(self, axis):
        return self.x if axis == 0 else self.y


def greet(place):
    barrier = pltpu.get_barrier_semaphore()
    peers = [place.sibling()]
    peers += [place.along_x(d) for d in (1, 2, 3)]
    peers += [place.along_y(d) for d in (1, 2, 3)]
    peers += [place.along_z(d) for d in range(1, 8)]
    for peer in peers:
        pl.semaphore_signal(barrier, inc=1, device_id=peer, device_id_type=MESH)
    return lambda: pl.semaphore_wait(barrier, len(peers))


def wrap8(value):
    return lax.rem(value + 16, 8)


class RingZ:
    def __init__(self, place, copies, base, part, slots, full):
        self.place, self.copies, self.base = place, copies, base
        self.part, self.slots, self.full = part, slots, full

    @staticmethod
    def box(way, quarter, dist):
        lead = (way > 0) == (quarter < 2)
        return (0 if way > 0 else 14) + (quarter % 2) * 7 + (dist - 1 if lead else 3 + dist)

    def push(self, way, quarter, dist):
        box = self.box(way, quarter, dist)
        chunk = wrap8(self.place.z + way * dist)
        self.copies.send(self.base + box, self.part.at[chunk, quarter], self.slots.at[box],
                         self.place.along_z(way))

    def pull(self, way, quarter, dist):
        box = self.box(way, quarter, dist)
        self.copies.arrived(self.base + box)
        chunk = wrap8(self.place.z + way * (dist - 1))
        self.part[chunk, quarter] = self.part[chunk, quarter] + self.slots[box]

    LEADS = ((1, 0), (-1, 2), (1, 1), (-1, 3))
    OTHERS = ((1, 2), (-1, 0), (1, 3), (-1, 1))

    def scatter_steps(self):
        for way, quarter in self.LEADS:
            self.push(way, quarter, 4)
        yield
        for way, quarter in self.OTHERS:
            self.push(way, quarter, 3)
        yield
        for step in range(3):
            for way, quarter in self.LEADS:
                self.pull(way, quarter, 4 - step)
                self.push(way, quarter, 3 - step)
            for way, quarter in self.OTHERS:
                self.pull(way, quarter, 3 - step)
                if step < 2:
                    self.push(way, quarter, 2 - step)
            yield
        z = self.place.z
        for way, quarter in self.LEADS:
            self.pull(way, quarter, 1)
            self.full[z, quarter] = self.part[z, quarter]
            for to in (1, -1):
                self.push_on(to, quarter, 0)
        yield

    def gather_slot(self, way, quarter, dist):
        return self.base + 28 + (0 if way > 0 else 14) + (quarter * 3 + dist if dist < 3 else 12 + quarter % 2)

    def push_on(self, way, quarter, dist):
        ref = self.full.at[wrap8(self.place.z - way * dist), quarter]
        self.copies.send(self.gather_slot(way, quarter, dist), ref, ref, self.place.along_z(way))

    def gather_steps(self, use):
        copies, slot, push, z = self.copies, self.gather_slot, self.push_on, self.place.z
        use(z)
        order = self.LEADS + self.OTHERS
        for dist in (1, 2):
            for way, quarter in order:
                copies.arrived(slot(way, quarter, dist - 1))
                push(way, quarter, dist)
            for way in (1, -1):
                use(wrap8(z + way * dist))
            yield
        for way, quarter in self.LEADS:
            copies.arrived(slot(way, quarter, 2))
            push(way, quarter, 3)
        for way, quarter in self.OTHERS:
            copies.arrived(slot(way, quarter, 2))
        for way in (1, -1):
            use(wrap8(z + way * 3))
        yield
        for way, quarter in self.LEADS:
            copies.arrived(slot(way, quarter, 3))
        use(wrap8(z + 4))
        yield


class SumRows:
    STREAMS = ((0, 0), (1, 0), (0, 1), (1, 1))

    def __init__(self, place, copies, base, part, from_core, from_line, from_point, full):
        self.place, self.copies, self.base = place, copies, base
        self.part, self.full = part, full
        self.from_core, self.from_line, self.from_point = from_core, from_line, from_point

    def slot(self, h, s, kind, d):
        return self.base + 17 * (2 * h + s) + kind + d

    def steps(self, use=None):
        place, copies, slot = self.place, self.copies, self.slot
        part, full, core = self.part, self.full, place.core
        first = [place.at(0), place.at(1)]
        second = [place.at(1), place.at(0)]
        CORE, LINE, POINT, POINT_BACK, LINE_BACK, BACK = 0, 0, 3, 6, 9, 13
        for h, s in self.STREAMS:
            copies.send(slot(h, s, CORE, 0), part.at[h, 1 - core, s], self.from_core.at[h, s], place.sibling())
        yield
        for h, s in self.STREAMS:
            copies.arrived(slot(h, s, CORE, 0))
            for d in (2, 1, 3, 0):
                at = lax.rem(first[h] + d, 4)
                part[h, core, s, at] = part[h, core, s, at] + self.from_core[h, s, at]
                if d:
                    copies.send(slot(h, s, LINE, d), part.at[h, core, s, at], self.from_line.at[h, s, d - 1],
                                place.line(h, d))
        yield
        for h, s in self.STREAMS:
            a = first[h]
            for d in (1, 2, 3):
                copies.arrived(slot(h, s, LINE, d))
            part[h, core, s, a] = (part[h, core, s, a] + self.from_line[h, s, 0]) + (
                self.from_line[h, s, 1] + self.from_line[h, s, 2])
            for d in (2, 1, 3):
                b = lax.rem(second[h] + d, 4)
                copies.send(slot(h, s, POINT, d), part.at[h, core, s, a, b], self.from_point.at[h, s, d - 1],
                            place.line(1 - h, d))
        yield
        for h, s in self.STREAMS:
            a, b = first[h], second[h]
            for d in (1, 2, 3):
                copies.arrived(slot(h, s, POINT, d))
            full[h, core, s, a, b] = (part[h, core, s, a, b] + self.from_point[h, s, 0]) + (
                self.from_point[h, s, 1] + self.from_point[h, s, 2])
            ref = full.at[h, core, s, a, b]
            for d in (2, 1, 3):
                copies.send(slot(h, s, POINT_BACK, d), ref, ref, place.line(1 - h, d))
        yield
        for h, s in self.STREAMS:
            for d in (1, 2, 3):
                copies.arrived(slot(h, s, POINT_BACK, d))
            ref = full.at[h, core, s, first[h]]
            for d in (2, 1, 3):
                copies.send(slot(h, s, LINE_BACK, d), ref, ref, place.line(h, d))
            copies.send(slot(h, s, BACK, 0), ref, ref, place.sibling())
        yield
        for h, s in self.STREAMS:
            for d in (1, 3, 2):
                copies.arrived(slot(h, s, LINE_BACK, d))
                ref = full.at[h, core, s, lax.rem(first[h] - d + 4, 4)]
                copies.send(slot(h, s, BACK, d), ref, ref, place.sibling())
        if use:
            use(core)
        yield
        for h, s in self.STREAMS:
            for d in range(4):
                copies.arrived(slot(h, s, BACK, d))
        if use:
            use(1 - core)
        yield


class SumAll:
    def __init__(self, place, copies, base, part, from_core, from_line, from_point, from_z, full):
        self.place, self.copies, self.base = place, copies, base
        self.part, self.full = part, full
        self.from_core, self.from_line, self.from_point, self.from_z = (
            from_core, from_line, from_point, from_z)

    def steps(self):
        place, copies, base = self.place, self.copies, self.base
        part, full, core, x, y = self.part, self.full, place.core, place.x, place.y
        copies.send(base, part.at[1 - core], self.from_core, place.sibling())
        yield
        copies.arrived(base)
        base += 1
        part[core] = part[core] + self.from_core[...]
        for d in (2, 1, 3):
            copies.send(base + d - 1, part.at[core, lax.rem(x + d, 4)], self.from_line.at[d - 1],
                        place.along_x(d))
        yield
        for d in (1, 2, 3):
            copies.arrived(base + d - 1)
        base += 3
        part[core, x] = (part[core, x] + self.from_line[0]) + (self.from_line[1] + self.from_line[2])
        for d in (2, 1, 3):
            copies.send(base + d - 1, part.at[core, x, lax.rem(y + d, 4)], self.from_point.at[d - 1],
                        place.along_y(d))
        yield
        for d in (1, 2, 3):
            copies.arrived(base + d - 1)
        base += 3
        mine = self.from_z.at[place.z]
        mine[...] = (part[core, x, y] + self.from_point[0]) + (self.from_point[1] + self.from_point[2])
        for d in (4, 3, 5, 2, 6, 1, 7):
            copies.send(base + d - 1, mine, mine, place.along_z(d))
        yield
        for d in range(1, 8):
            copies.arrived(base + d - 1)
        base += 7
        total = self.from_z[0]
        for z in range(1, 8):
            total = total + self.from_z[z]
        full[core, x, y] = total
        ref = full.at[core, x, y]
        for d in (2, 1, 3):
            copies.send(base + d - 1, ref, ref, place.along_y(d))
        yield
        for d in (1, 2, 3):
            copies.arrived(base + d - 1)
        base += 3
        ref = full.at[core, x]
        for d in (2, 1, 3):
            copies.send(base + d - 1, ref, ref, place.along_x(d))
        yield
        for d in (1, 2, 3):
            copies.arrived(base + d - 1)
        base += 3
        ref = full.at[core]
        copies.send(base, ref, ref, place.sibling())
        yield
        copies.arrived(base)
        yield


def run(steps):
    for _ in steps:
        pass


def interleave(*many):
    live = list(many)
    while live:
        live = [one for one in live if next(one, run) is None]


def multiply(x_hi, x_lo, t_hi, t_lo, store, i):
    rows = pl.ds(pl.multiple_of(i * 256, 256), 256)
    dot = functools.partial(jnp.dot, preferred_element_type=F32)
    for j in range(2):
        lanes = pl.ds(j * 256, 256)
        xh, xl = x_hi[rows, :], x_lo[rows, :]
        th, tl = t_hi[:, lanes], t_lo[:, lanes]
        store(i, j, dot(xh, th) + (dot(xh, tl) + dot(xl, th)))


def dots(lefts, rights):
    terms = [left * right for left, right in zip(lefts, rights)]
    while len(terms) > 1:
        terms = [sum(terms[i + 1:i + 2], terms[i]) for i in range(0, len(terms), 2)]
    return terms[0]


def inverse_factor(ref, start, hook):
    groups = [ref[start + 8 * g:start + 8 * g + 8, start:start + 128] for g in range(16)]
    wide = (8, 128)
    lane = lax.broadcasted_iota(jnp.int32, wide, 1)
    sub = lax.broadcasted_iota(jnp.int32, wide, 0)

    def row(value, k):
        return jnp.broadcast_to(value[k:k + 1, :], wide)

    def col(value, k):
        return jnp.broadcast_to(value[:, k:k + 1], wide)

    for g in range(16):
        at = 8 * g
        inside = (lane >= at) & (lane < at + 8)
        own = groups[g]
        c = [col(own, at + k) for k in range(8)]
        u = jnp.where(inside, jnp.where(lane == at + sub, 1.0, 0.0), own)
        inverse = root = jnp.zeros(wide, F32)
        for k in range(8):
            pivot = row(c[k], k)
            inv = 1.0 / pivot
            inverse = jnp.where(sub == k, inv, inverse)
            root = jnp.where(sub == k, lax.rsqrt(pivot), root)
            if k < 7:
                f = jnp.where(sub > k, c[k], 0.0) * inv
                for m in range(k + 1, 8):
                    c[m] = c[m] - f * row(c[m], k)
                u = u - f * row(u, k)
        ref[start + at:start + at + 8, start:start + 128] = jnp.where(lane <= at + sub, u * root, 0.0)
        hook((start + at) // 8)
        if g == 15:
            break
        q = u * inverse
        for m in range(7, 0, -1):
            q = q - jnp.where(sub < m, c[m] * inverse, 0.0) * row(q, m)
        rows = [row(q, k) for k in range(8)]
        near = min(g + 3, 16)
        if near < 16:
            below = jnp.concatenate(groups[near:], 0)
            zeros = [jnp.zeros((at, 128), F32)] if g else []
            step = jnp.concatenate(zeros + [q, jnp.zeros((120 - at, 128), F32)], 0)
            change = jnp.dot(below, step, precision=HI, preferred_element_type=F32)
        for v in range(g + 1, near):
            cols = [col(groups[v], at + k) for k in range(8)]
            groups[v] = jnp.where(inside, 0.0, groups[v]) - dots(cols, rows)
        for v in range(near, 16):
            groups[v] = jnp.where(inside, 0.0, groups[v]) - change[8 * (v - near):8 * (v - near) + 8]


def factor(m_ref, hook):
    dot = functools.partial(jnp.dot, precision=HI, preferred_element_type=F32)
    for k in range(4):
        at = 128 * k
        inverse_factor(m_ref, at, hook)
        w = m_ref[at:at + 128, at:at + 128]
        if k > 0:
            m_ref[at:at + 128, :at] = dot(w, m_ref[at:at + 128, :at])
        if k < 3:
            u = dot(w, m_ref[at:at + 128, at + 128:])
            ut = u.T
            m_ref[at + 128:, at + 128:] = m_ref[at + 128:, at + 128:] - dot(ut, u)
            if k > 0:
                m_ref[at + 128:, :at] = m_ref[at + 128:, :at] - dot(ut, m_ref[at:at + 128, :at])
            m_ref[at + 128:, at:at + 128] = -dot(ut, w)
            m_ref[at:at + 128, at + 128:] = jnp.zeros((128, 384 - at), F32)


def set_gram(packed, m_ref):
    row = lax.broadcasted_iota(jnp.int32, (256, 256), 0)
    col = lax.broadcasted_iota(jnp.int32, (256, 256), 1)
    turned = packed.T
    gram_r = jnp.where(row >= col, packed, turned)
    gram_i = jnp.where(row < col, packed, jnp.where(row > col, -turned, 0.0))
    m_ref[:256, :256] = gram_r
    m_ref[256:, 256:] = gram_r
    m_ref[256:, :256] = gram_i
    m_ref[:256, 256:] = -gram_i


def finish_kernel(scale, y_ref, b_ref, m_ref, basis_ref, proj_ref, l_hi, l_lo, basis, proj, sems):
    for i in range(4):
        rows = slice(128 * i, 128 * i + 128)
        l_hi[rows, :], l_lo[rows, :] = split(m_ref[rows, :])

    def product(left_hi, left_lo, right_hi, right_lo):
        dot = functools.partial(
            lax.dot_general, dimension_numbers=(((1,), (1,)), ((), ())), preferred_element_type=F32)
        return dot(left_hi, right_hi) + (dot(left_hi, right_lo) + dot(left_lo, right_hi))

    copies = []

    def out(ref, tile, p, rows, value):
        tile[p, rows, :] = value
        copy = pltpu.make_async_copy(tile.at[p, rows], ref.at[p, rows], sems.at[len(copies)])
        copy.start()
        copies.append(copy)

    for i in range(2):
        rows = pl.ds(i * 256, 256)
        real, imag = y_ref[rows, :256], y_ref[rows, 256:]
        for p, pair in enumerate(((real, -imag), (imag, real))):
            value = product(*split(jnp.concatenate(pair, 1)), l_hi[...], l_lo[...]) * scale
            out(basis_ref, basis, p, rows, value)
    real, imag = b_ref[0], b_ref[1]
    for p, pair in enumerate(((real, -imag), (imag, real))):
        hi, lo = split(jnp.concatenate(pair, 1))
        for i in range(2):
            rows = pl.ds(i * 256, 256)
            out(proj_ref, proj, p, rows, product(l_hi[rows, :], l_lo[rows, :], hi, lo))
    for copy in copies:
        copy.wait()


def finish(y, b, inverse, scale):
    vmem = pl.BlockSpec(memory_space=pltpu.VMEM)
    return pl.pallas_call(
        functools.partial(finish_kernel, scale),
        out_shape=(jax.ShapeDtypeStruct((2, 512, 512), F32),) * 2,
        in_specs=[vmem] * 3,
        out_specs=(pl.BlockSpec(memory_space=pl.ANY),) * 2,
        scratch_shapes=[
            *[pltpu.VMEM((512, 512), BF16)] * 2,
            *[pltpu.VMEM((2, 512, 512), F32)] * 2,
            pltpu.SemaphoreType.DMA((8,)),
        ],
        compiler_params=pltpu.CompilerParams(vmem_limit_bytes=48 * 2**20),
        name="finish",
    )(y, b, inverse)

ORDER = "ggygygygybgtgg"
HOOKS = (3, 14, 25, 38, 48)


def power_kernel(a_hbm, s_hbm, y_ref, b_ref, m_ref, x_hi, x_lo, xt_hi, xt_lo, t_hi, t_lo,
                 z_part, z_slots, z_full, z_part2, z_slots2,
                 r_part, r_core, r_line, r_point, r_full, r_part2, r_core2, r_line2, r_point2,
                 g_ref, g_part, g_core, g_line, g_point, g_z, a_ref, s_ref, in_sem, send_sem, recv_sem):
    place = Place()
    all_here = greet(place)
    copies = Copies(send_sem, recv_sem)

    def set_pair(rows, real, imag, sign):
        low = pl.ds(rows, real.shape[0])
        high = pl.ds(512 + rows, real.shape[0])
        for at, lanes, value in (
            (low, slice(0, 256), real), (low, slice(256, 512), imag),
            (high, slice(0, 256), sign * imag), (high, slice(256, 512), -sign * real),
        ):
            t_hi[at, lanes], t_lo[at, lanes] = split(value)

    fetches = [
        pltpu.make_async_copy(src, dst, in_sem.at[n])
        for n, (src, dst) in enumerate(((s_hbm, s_ref), (a_hbm, a_ref)))
    ]
    for fetch in fetches:
        fetch.start()
    fetches[0].wait()

    @pl.loop(0, 8)
    def _(i):
        rows = pl.ds(i * 64, 64)
        set_pair(i * 64, s_ref[0, rows, :], s_ref[1, rows, :], -1.0)

    fetches[1].wait()

    @pl.loop(0, 8)
    def _(i):
        rows = pl.ds(i * 64, 64)
        for p in (0, 1):
            x_hi[rows, p * 512:(p + 1) * 512], x_lo[rows, p * 512:(p + 1) * 512] = split(a_ref[p, rows, :])

    def store_chunks(ref):
        def store(i, j, tile):
            ref[pl.ds(i * 4, 4), :, :, j * 256:(j + 1) * 256] = tile.reshape(4, 4, 16, 256)
        return store

    def store_rows(ref):
        def store(i, j, tile):
            ref[j, i] = tile.reshape(2, 4, 4, 8, 256)
        return store

    far = 1 - place.z // 4
    ring = RingZ(place, copies, 0, z_part, z_slots, z_full)
    steps = ring.scatter_steps()
    multiply(x_hi, x_lo, t_hi, t_lo, store_chunks(z_part), far)
    all_here()
    next(steps)
    multiply(x_hi, x_lo, t_hi, t_lo, store_chunks(z_part), 1 - far)
    next(steps)

    @pl.loop(0, 4)
    def _(i):
        for p in (0, 1):
            rows = pl.ds(i * 128, 128)
            block = a_ref[p, :, rows].T
            lanes = slice(p * 512, (p + 1) * 512)
            xt_hi[rows, lanes], xt_lo[rows, lanes] = split(block)

    run(steps)

    def chunk_to_t(ref):
        def use(chunk):
            value = ref[chunk].reshape(64, 512)
            set_pair(pl.multiple_of(chunk * 64, 64), value[:, :256], value[:, 256:], 1.0)
        return use

    run(ring.gather_steps(chunk_to_t(z_full)))
    multiply(xt_hi, xt_lo, t_hi, t_lo, store_rows(r_part), 1 - place.core)

    def rows_to_t(k):
        @pl.loop(0, 4)
        def _(i):
            s, lines = i // 2, pl.ds(lax.rem(i, 2) * 2, 2)
            set_pair(pl.multiple_of(k * 256 + i * 64, 64), r_full[0, k, s, lines].reshape(64, 256),
                     r_full[1, k, s, lines].reshape(64, 256), -1.0)

    steps = SumRows(place, copies, Z_SLOTS, r_part, r_core, r_line, r_point, r_full).steps(rows_to_t)
    next(steps)
    multiply(xt_hi, xt_lo, t_hi, t_lo, store_rows(r_part), place.core)
    run(steps)

    ring = RingZ(place, copies, Z_SLOTS + ROW_SLOTS, z_part2, z_slots2, y_ref)
    steps = ring.scatter_steps()
    multiply(x_hi, x_lo, t_hi, t_lo, store_chunks(z_part2), far)
    next(steps)
    multiply(x_hi, x_lo, t_hi, t_lo, store_chunks(z_part2), 1 - far)
    run(steps)
    mine = z_part2[place.z].reshape(64, 512)
    steps = ring.gather_steps(chunk_to_t(y_ref))
    real, imag = mine[:, :256], mine[:, 256:]
    tall = jnp.concatenate([real, imag], 0).T
    gram_r = jnp.dot(tall, jnp.concatenate([real, imag], 0), precision=HI, preferred_element_type=F32)
    gram_i = jnp.dot(tall, jnp.concatenate([imag, -real], 0), precision=HI, preferred_element_type=F32)
    low = lax.broadcasted_iota(jnp.int32, (256, 256), 0) >= lax.broadcasted_iota(jnp.int32, (256, 256), 1)
    g_part[...] = jnp.where(low, gram_r, gram_i).reshape(2, 4, 4, 8, 256)
    gram_steps = SumAll(place, copies, 2 * Z_SLOTS + ROW_SLOTS, g_part, g_core, g_line, g_point, g_z, g_ref).steps()
    tail = SumRows(place, copies, 2 * Z_SLOTS + ROW_SLOTS + GRAM_SLOTS, r_part2, r_core2, r_line2,
                   r_point2, b_ref).steps()

    def start_b():
        multiply(xt_hi, xt_lo, t_hi, t_lo, store_rows(r_part2), 1 - place.core)
        next(tail)
        multiply(xt_hi, xt_lo, t_hi, t_lo, store_rows(r_part2), place.core)

    for turn in ORDER:
        if turn == "g":
            next(gram_steps)
        elif turn == "y":
            next(steps)
        elif turn == "b":
            start_b()
        else:
            next(tail)

    def hook(done):
        if done in HOOKS:
            next(tail)

    set_gram(g_ref[...].reshape(256, 256), m_ref)
    factor(m_ref, hook)
    run(tail)
    copies.finish()


def power(samples, sketch):
    vmem = pl.BlockSpec(memory_space=pltpu.VMEM)
    slots = 2 * Z_SLOTS + 2 * ROW_SLOTS + GRAM_SLOTS
    chunks = pltpu.VMEM((8, 4, 16, 512), F32)
    boxes = pltpu.VMEM((28, 16, 512), F32)
    rows = [
        pltpu.VMEM((2, 2, 2, 4, 4, 8, 256), F32),
        pltpu.VMEM((2, 2, 4, 4, 8, 256), F32),
        pltpu.VMEM((2, 2, 3, 4, 8, 256), F32),
        pltpu.VMEM((2, 2, 3, 8, 256), F32),
    ]
    return pl.pallas_call(
        power_kernel,
        out_shape=(
            jax.ShapeDtypeStruct((8, 4, 16, 512), F32),
            jax.ShapeDtypeStruct((2, 2, 2, 4, 4, 8, 256), F32),
            jax.ShapeDtypeStruct((512, 512), F32),
        ),
        in_specs=[pl.BlockSpec(memory_space=pl.ANY)] * 2,
        out_specs=(vmem,) * 3,
        scratch_shapes=[
            *[pltpu.VMEM((512, 1024), BF16)] * 4,
            *[pltpu.VMEM((1024, 512), BF16)] * 2,
            chunks, boxes, chunks, chunks, boxes,
            *rows, pltpu.VMEM((2, 2, 2, 4, 4, 8, 256), F32), *rows,
            *[pltpu.VMEM((2, 4, 4, 8, 256), F32)] * 2,
            pltpu.VMEM((4, 4, 8, 256), F32),
            pltpu.VMEM((3, 4, 8, 256), F32),
            pltpu.VMEM((3, 8, 256), F32),
            pltpu.VMEM((8, 8, 256), F32),
            pltpu.VMEM((2, 512, 512), F32),
            pltpu.VMEM((2, 512, 256), F32),
            pltpu.SemaphoreType.DMA((2,)),
            *[pltpu.SemaphoreType.DMA((slots,))] * 2,
        ],
        compiler_params=pltpu.CompilerParams(
            collective_id=0, has_side_effects=True, vmem_limit_bytes=50 * 2**20
        ),
        name="power",
    )(samples, sketch)


def per_device(samples, sketch):
    y, b, inverse = power(samples, sketch)
    total_rows = samples.shape[1] * lax.axis_size("rows")
    scale = float(np.sqrt(np.float32(2 * total_rows)))
    return finish(y.reshape(512, 512), b.reshape(2, 512, 256), inverse, scale)


def solution(mesh):
    placed = (P(None, "rows", "cols"), P(None, "cols", None))
    return jax.shard_map(
        per_device,
        mesh=mesh,
        in_specs=placed,
        out_specs=(P(None, "rows", None), P(None, None, "cols")),
        check_vma=False,
    )
```

```python
import functools

import jax
import jax.numpy as jnp
import numpy as np
from jax import lax
from jax.experimental import pallas as pl
from jax.experimental.pallas import tpu as pltpu
from jax.sharding import PartitionSpec as P

MESH = pl.DeviceIdType.MESH
HI = lax.Precision.HIGHEST
F32 = jnp.float32
BF16 = jnp.bfloat16

Z_SLOTS = 56
ROW_SLOTS = 68
GRAM_SLOTS = 21


def split(value):
    high = value.astype(BF16)
    return high, (value - high.astype(F32)).astype(BF16)


class Copies:
    def __init__(self, send_sem, recv_sem):
        self.send_sem, self.recv_sem = send_sem, recv_sem
        self.made = {}

    def send(self, slot, src, dst, device):
        copy = pltpu.make_async_remote_copy(
            src_ref=src, dst_ref=dst, send_sem=self.send_sem.at[slot],
            recv_sem=self.recv_sem.at[slot], device_id=device, device_id_type=MESH,
        )
        copy.start()
        self.made[slot] = copy

    def arrived(self, slot):
        self.made[slot].wait_recv()

    def finish(self):
        for copy in self.made.values():
            copy.wait_send()


class Place:
    def __init__(self):
        self.r = lax.axis_index("rows")
        self.z = lax.axis_index("cols")
        self.core = lax.rem(self.r, 2)
        self.x = lax.rem(self.r // 2, 4)
        self.y = self.r // 8

    def along_z(self, d):
        return (self.r, lax.rem(self.z + d + 8, 8))

    def along_x(self, d):
        return ((self.y * 4 + lax.rem(self.x + d, 4)) * 2 + self.core, self.z)

    def along_y(self, d):
        return ((lax.rem(self.y + d, 4) * 4 + self.x) * 2 + self.core, self.z)

    def sibling(self):
        return (self.r + 1 - 2 * self.core, self.z)

    def line(self, axis, d):
        return self.along_x(d) if axis == 0 else self.along_y(d)

    def at(self, axis):
        return self.x if axis == 0 else self.y


def greet(place):
    barrier = pltpu.get_barrier_semaphore()
    peers = [place.sibling()]
    peers += [place.along_x(d) for d in (1, 2, 3)]
    peers += [place.along_y(d) for d in (1, 2, 3)]
    peers += [place.along_z(d) for d in range(1, 8)]
    for peer in peers:
        pl.semaphore_signal(barrier, inc=1, device_id=peer, device_id_type=MESH)
    return lambda: pl.semaphore_wait(barrier, len(peers))


def wrap8(value):
    return lax.rem(value + 16, 8)


class RingZ:
    def __init__(self, place, copies, base, part, slots, full):
        self.place, self.copies, self.base = place, copies, base
        self.part, self.slots, self.full = part, slots, full

    @staticmethod
    def box(way, quarter, dist):
        lead = (way > 0) == (quarter < 2)
        return (0 if way > 0 else 14) + (quarter % 2) * 7 + (dist - 1 if lead else 3 + dist)

    def push(self, way, quarter, dist):
        box = self.box(way, quarter, dist)
        chunk = wrap8(self.place.z + way * dist)
        self.copies.send(self.base + box, self.part.at[chunk, quarter], self.slots.at[box],
                         self.place.along_z(way))

    def pull(self, way, quarter, dist):
        box = self.box(way, quarter, dist)
        self.copies.arrived(self.base + box)
        chunk = wrap8(self.place.z + way * (dist - 1))
        self.part[chunk, quarter] = self.part[chunk, quarter] + self.slots[box]

    LEADS = ((1, 0), (-1, 2), (1, 1), (-1, 3))
    OTHERS = ((1, 2), (-1, 0), (1, 3), (-1, 1))

    def scatter_steps(self):
        for way, quarter in self.LEADS:
            self.push(way, quarter, 4)
        yield
        for way, quarter in self.OTHERS:
            self.push(way, quarter, 3)
        yield
        for step in range(3):
            for way, quarter in self.LEADS:
                self.pull(way, quarter, 4 - step)
                self.push(way, quarter, 3 - step)
            for way, quarter in self.OTHERS:
                self.pull(way, quarter, 3 - step)
                if step < 2:
                    self.push(way, quarter, 2 - step)
            yield
        z = self.place.z
        for way, quarter in self.LEADS:
            self.pull(way, quarter, 1)
            self.full[z, quarter] = self.part[z, quarter]
            for to in (1, -1):
                self.push_on(to, quarter, 0)
        yield

    def gather_slot(self, way, quarter, dist):
        return self.base + 28 + (0 if way > 0 else 14) + (quarter * 3 + dist if dist < 3 else 12 + quarter % 2)

    def push_on(self, way, quarter, dist):
        ref = self.full.at[wrap8(self.place.z - way * dist), quarter]
        self.copies.send(self.gather_slot(way, quarter, dist), ref, ref, self.place.along_z(way))

    def gather_steps(self, use):
        copies, slot, push, z = self.copies, self.gather_slot, self.push_on, self.place.z
        use(z)
        order = self.LEADS + self.OTHERS
        for dist in (1, 2):
            for way, quarter in order:
                copies.arrived(slot(way, quarter, dist - 1))
                push(way, quarter, dist)
            for way in (1, -1):
                use(wrap8(z + way * dist))
            yield
        for way, quarter in self.LEADS:
            copies.arrived(slot(way, quarter, 2))
            push(way, quarter, 3)
        for way, quarter in self.OTHERS:
            copies.arrived(slot(way, quarter, 2))
        for way in (1, -1):
            use(wrap8(z + way * 3))
        yield
        for way, quarter in self.LEADS:
            copies.arrived(slot(way, quarter, 3))
        use(wrap8(z + 4))
        yield


class SumRows:
    STREAMS = ((0, 0), (1, 0), (0, 1), (1, 1))

    def __init__(self, place, copies, base, part, from_core, from_line, from_point, full):
        self.place, self.copies, self.base = place, copies, base
        self.part, self.full = part, full
        self.from_core, self.from_line, self.from_point = from_core, from_line, from_point

    def slot(self, h, s, kind, d):
        return self.base + 17 * (2 * h + s) + kind + d

    def steps(self, use=None):
        place, copies, slot = self.place, self.copies, self.slot
        part, full, core = self.part, self.full, place.core
        first = [place.at(0), place.at(1)]
        second = [place.at(1), place.at(0)]
        CORE, LINE, POINT, POINT_BACK, LINE_BACK, BACK = 0, 0, 3, 6, 9, 13
        for h, s in self.STREAMS:
            copies.send(slot(h, s, CORE, 0), part.at[h, 1 - core, s], self.from_core.at[h, s], place.sibling())
        yield
        for h, s in self.STREAMS:
            copies.arrived(slot(h, s, CORE, 0))
            for d in (2, 1, 3, 0):
                at = lax.rem(first[h] + d, 4)
                part[h, core, s, at] = part[h, core, s, at] + self.from_core[h, s, at]
                if d:
                    copies.send(slot(h, s, LINE, d), part.at[h, core, s, at], self.from_line.at[h, s, d - 1],
                                place.line(h, d))
        yield
        for h, s in self.STREAMS:
            a = first[h]
            for d in (1, 2, 3):
                copies.arrived(slot(h, s, LINE, d))
            part[h, core, s, a] = (part[h, core, s, a] + self.from_line[h, s, 0]) + (
                self.from_line[h, s, 1] + self.from_line[h, s, 2])
            for d in (2, 1, 3):
                b = lax.rem(second[h] + d, 4)
                copies.send(slot(h, s, POINT, d), part.at[h, core, s, a, b], self.from_point.at[h, s, d - 1],
                            place.line(1 - h, d))
        yield
        for h, s in self.STREAMS:
            a, b = first[h], second[h]
            for d in (1, 2, 3):
                copies.arrived(slot(h, s, POINT, d))
            full[h, core, s, a, b] = (part[h, core, s, a, b] + self.from_point[h, s, 0]) + (
                self.from_point[h, s, 1] + self.from_point[h, s, 2])
            ref = full.at[h, core, s, a, b]
            for d in (2, 1, 3):
                copies.send(slot(h, s, POINT_BACK, d), ref, ref, place.line(1 - h, d))
        yield
        for h, s in self.STREAMS:
            for d in (1, 2, 3):
                copies.arrived(slot(h, s, POINT_BACK, d))
            ref = full.at[h, core, s, first[h]]
            for d in (2, 1, 3):
                copies.send(slot(h, s, LINE_BACK, d), ref, ref, place.line(h, d))
            copies.send(slot(h, s, BACK, 0), ref, ref, place.sibling())
        yield
        for h, s in self.STREAMS:
            for d in (1, 3, 2):
                copies.arrived(slot(h, s, LINE_BACK, d))
                ref = full.at[h, core, s, lax.rem(first[h] - d + 4, 4)]
                copies.send(slot(h, s, BACK, d), ref, ref, place.sibling())
        if use:
            use(core)
        yield
        for h, s in self.STREAMS:
            for d in range(4):
                copies.arrived(slot(h, s, BACK, d))
        if use:
            use(1 - core)
        yield


class SumAll:
    def __init__(self, place, copies, base, part, from_core, from_line, from_point, from_z, full):
        self.place, self.copies, self.base = place, copies, base
        self.part, self.full = part, full
        self.from_core, self.from_line, self.from_point, self.from_z = (
            from_core, from_line, from_point, from_z)

    def steps(self):
        place, copies, base = self.place, self.copies, self.base
        part, full, core, x, y = self.part, self.full, place.core, place.x, place.y
        copies.send(base, part.at[1 - core], self.from_core, place.sibling())
        yield
        copies.arrived(base)
        base += 1
        part[core] = part[core] + self.from_core[...]
        for d in (2, 1, 3):
            copies.send(base + d - 1, part.at[core, lax.rem(x + d, 4)], self.from_line.at[d - 1],
                        place.along_x(d))
        yield
        for d in (1, 2, 3):
            copies.arrived(base + d - 1)
        base += 3
        part[core, x] = (part[core, x] + self.from_line[0]) + (self.from_line[1] + self.from_line[2])
        for d in (2, 1, 3):
            copies.send(base + d - 1, part.at[core, x, lax.rem(y + d, 4)], self.from_point.at[d - 1],
                        place.along_y(d))
        yield
        for d in (1, 2, 3):
            copies.arrived(base + d - 1)
        base += 3
        mine = self.from_z.at[place.z]
        mine[...] = (part[core, x, y] + self.from_point[0]) + (self.from_point[1] + self.from_point[2])
        for d in (4, 3, 5, 2, 6, 1, 7):
            copies.send(base + d - 1, mine, mine, place.along_z(d))
        yield
        for d in range(1, 8):
            copies.arrived(base + d - 1)
        base += 7
        total = self.from_z[0]
        for z in range(1, 8):
            total = total + self.from_z[z]
        full[core, x, y] = total
        ref = full.at[core, x, y]
        for d in (2, 1, 3):
            copies.send(base + d - 1, ref, ref, place.along_y(d))
        yield
        for d in (1, 2, 3):
            copies.arrived(base + d - 1)
        base += 3
        ref = full.at[core, x]
        for d in (2, 1, 3):
            copies.send(base + d - 1, ref, ref, place.along_x(d))
        yield
        for d in (1, 2, 3):
            copies.arrived(base + d - 1)
        base += 3
        ref = full.at[core]
        copies.send(base, ref, ref, place.sibling())
        yield
        copies.arrived(base)
        yield


def run(steps):
    for _ in steps:
        pass


def interleave(*many):
    live = list(many)
    while live:
        live = [one for one in live if next(one, run) is None]


def multiply(x_hi, x_lo, t_hi, t_lo, store, i):
    rows = pl.ds(pl.multiple_of(i * 256, 256), 256)
    dot = functools.partial(jnp.dot, preferred_element_type=F32)
    for j in range(2):
        lanes = pl.ds(j * 256, 256)
        xh, xl = x_hi[rows, :], x_lo[rows, :]
        th, tl = t_hi[:, lanes], t_lo[:, lanes]
        store(i, j, dot(xh, th) + (dot(xh, tl) + dot(xl, th)))


def dots(lefts, rights):
    terms = [left * right for left, right in zip(lefts, rights)]
    while len(terms) > 1:
        terms = [sum(terms[i + 1:i + 2], terms[i]) for i in range(0, len(terms), 2)]
    return terms[0]


def inverse_factor(ref, start, hook):
    groups = [ref[start + 8 * g:start + 8 * g + 8, start:start + 128] for g in range(16)]
    wide = (8, 128)
    lane = lax.broadcasted_iota(jnp.int32, wide, 1)
    sub = lax.broadcasted_iota(jnp.int32, wide, 0)

    def row(value, k):
        return jnp.broadcast_to(value[k:k + 1, :], wide)

    def col(value, k):
        return jnp.broadcast_to(value[:, k:k + 1], wide)

    for g in range(16):
        at = 8 * g
        inside = (lane >= at) & (lane < at + 8)
        own = groups[g]
        c = [col(own, at + k) for k in range(8)]
        u = jnp.where(inside, jnp.where(lane == at + sub, 1.0, 0.0), own)
        inverse = root = jnp.zeros(wide, F32)
        for k in range(8):
            pivot = row(c[k], k)
            inv = 1.0 / pivot
            inverse = jnp.where(sub == k, inv, inverse)
            root = jnp.where(sub == k, lax.rsqrt(pivot), root)
            if k < 7:
                f = jnp.where(sub > k, c[k], 0.0) * inv
                for m in range(k + 1, 8):
                    c[m] = c[m] - f * row(c[m], k)
                u = u - f * row(u, k)
        ref[start + at:start + at + 8, start:start + 128] = jnp.where(lane <= at + sub, u * root, 0.0)
        hook((start + at) // 8)
        if g == 15:
            break
        q = u * inverse
        for m in range(7, 0, -1):
            q = q - jnp.where(sub < m, c[m] * inverse, 0.0) * row(q, m)
        rows = [row(q, k) for k in range(8)]
        near = min(g + 3, 16)
        if near < 16:
            below = jnp.concatenate(groups[near:], 0)
            zeros = [jnp.zeros((at, 128), F32)] if g else []
            step = jnp.concatenate(zeros + [q, jnp.zeros((120 - at, 128), F32)], 0)
            change = jnp.dot(below, step, precision=HI, preferred_element_type=F32)
        for v in range(g + 1, near):
            cols = [col(groups[v], at + k) for k in range(8)]
            groups[v] = jnp.where(inside, 0.0, groups[v]) - dots(cols, rows)
        for v in range(near, 16):
            groups[v] = jnp.where(inside, 0.0, groups[v]) - change[8 * (v - near):8 * (v - near) + 8]


def factor(m_ref, hook):
    dot = functools.partial(jnp.dot, precision=HI, preferred_element_type=F32)
    for k in range(4):
        at = 128 * k
        inverse_factor(m_ref, at, hook)
        w = m_ref[at:at + 128, at:at + 128]
        if k > 0:
            m_ref[at:at + 128, :at] = dot(w, m_ref[at:at + 128, :at])
        if k < 3:
            u = dot(w, m_ref[at:at + 128, at + 128:])
            ut = u.T
            m_ref[at + 128:, at + 128:] = m_ref[at + 128:, at + 128:] - dot(ut, u)
            if k > 0:
                m_ref[at + 128:, :at] = m_ref[at + 128:, :at] - dot(ut, m_ref[at:at + 128, :at])
            m_ref[at + 128:, at:at + 128] = -dot(ut, w)
            m_ref[at:at + 128, at + 128:] = jnp.zeros((128, 384 - at), F32)


def set_gram(packed, m_ref):
    row = lax.broadcasted_iota(jnp.int32, (256, 256), 0)
    col = lax.broadcasted_iota(jnp.int32, (256, 256), 1)
    turned = packed.T
    gram_r = jnp.where(row >= col, packed, turned)
    gram_i = jnp.where(row < col, packed, jnp.where(row > col, -turned, 0.0))
    m_ref[:256, :256] = gram_r
    m_ref[256:, 256:] = gram_r
    m_ref[256:, :256] = gram_i
    m_ref[:256, 256:] = -gram_i


def finish_kernel(scale, y_ref, b_ref, m_ref, basis_ref, proj_ref, l_hi, l_lo, basis, proj, sems):
    for i in range(4):
        rows = slice(128 * i, 128 * i + 128)
        l_hi[rows, :], l_lo[rows, :] = split(m_ref[rows, :])

    def product(left_hi, left_lo, right_hi, right_lo):
        dot = functools.partial(
            lax.dot_general, dimension_numbers=(((1,), (1,)), ((), ())), preferred_element_type=F32)
        return dot(left_hi, right_hi) + (dot(left_hi, right_lo) + dot(left_lo, right_hi))

    copies = []

    def out(ref, tile, p, rows, value):
        tile[p, rows, :] = value
        copy = pltpu.make_async_copy(tile.at[p, rows], ref.at[p, rows], sems.at[len(copies)])
        copy.start()
        copies.append(copy)

    for i in range(2):
        rows = pl.ds(i * 256, 256)
        real, imag = y_ref[rows, :256], y_ref[rows, 256:]
        for p, pair in enumerate(((real, -imag), (imag, real))):
            value = product(*split(jnp.concatenate(pair, 1)), l_hi[...], l_lo[...]) * scale
            out(basis_ref, basis, p, rows, value)
    real, imag = b_ref[0], b_ref[1]
    for p, pair in enumerate(((real, -imag), (imag, real))):
        hi, lo = split(jnp.concatenate(pair, 1))
        for i in range(2):
            rows = pl.ds(i * 256, 256)
            out(proj_ref, proj, p, rows, product(l_hi[rows, :], l_lo[rows, :], hi, lo))
    for copy in copies:
        copy.wait()


def finish(y, b, inverse, scale):
    vmem = pl.BlockSpec(memory_space=pltpu.VMEM)
    return pl.pallas_call(
        functools.partial(finish_kernel, scale),
        out_shape=(jax.ShapeDtypeStruct((2, 512, 512), F32),) * 2,
        in_specs=[vmem] * 3,
        out_specs=(pl.BlockSpec(memory_space=pl.ANY),) * 2,
        scratch_shapes=[
            *[pltpu.VMEM((512, 512), BF16)] * 2,
            *[pltpu.VMEM((2, 512, 512), F32)] * 2,
            pltpu.SemaphoreType.DMA((8,)),
        ],
        compiler_params=pltpu.CompilerParams(vmem_limit_bytes=48 * 2**20),
        name="finish",
    )(y, b, inverse)

ORDER = "ggygygygybgtgg"
HOOKS = (3, 14, 25, 38, 48)


def power_kernel(a_hbm, s_hbm, y_ref, b_ref, m_ref, x_hi, x_lo, xt_hi, xt_lo, t_hi, t_lo,
                 z_part, z_slots, z_full, z_part2, z_slots2,
                 r_part, r_core, r_line, r_point, r_full, r_part2, r_core2, r_line2, r_point2,
                 g_ref, g_part, g_core, g_line, g_point, g_z, a_ref, s_ref, in_sem, send_sem, recv_sem):
    place = Place()
    all_here = greet(place)
    copies = Copies(send_sem, recv_sem)

    def set_pair(rows, real, imag, sign):
        low = pl.ds(rows, real.shape[0])
        high = pl.ds(512 + rows, real.shape[0])
        for at, lanes, value in (
            (low, slice(0, 256), real), (low, slice(256, 512), imag),
            (high, slice(0, 256), sign * imag), (high, slice(256, 512), -sign * real),
        ):
            t_hi[at, lanes], t_lo[at, lanes] = split(value)

    far = 1 - place.z // 4

    def tile_rows(i):
        return pl.ds(pl.multiple_of(i * 256, 256), 256)

    fetches = [
        pltpu.make_async_copy(s_hbm, s_ref, in_sem.at[0]),
        pltpu.make_async_copy(a_hbm.at[:, tile_rows(far)], a_ref.at[:, tile_rows(far)], in_sem.at[1]),
        pltpu.make_async_copy(a_hbm.at[:, tile_rows(1 - far)], a_ref.at[:, tile_rows(1 - far)], in_sem.at[2]),
    ]
    for fetch in fetches:
        fetch.start()
    fetches[0].wait()

    @pl.loop(0, 8)
    def _(i):
        rows = pl.ds(i * 64, 64)
        set_pair(i * 64, s_ref[0, rows, :], s_ref[1, rows, :], -1.0)

    def split_tile(tile):
        @pl.loop(0, 4)
        def _(i):
            rows = pl.ds(pl.multiple_of(tile * 256 + i * 64, 64), 64)
            for p in (0, 1):
                x_hi[rows, p * 512:(p + 1) * 512], x_lo[rows, p * 512:(p + 1) * 512] = split(a_ref[p, rows, :])

    fetches[1].wait()
    split_tile(far)

    def store_chunks(ref):
        def store(i, j, tile):
            ref[pl.ds(i * 4, 4), :, :, j * 256:(j + 1) * 256] = tile.reshape(4, 4, 16, 256)
        return store

    def store_rows(ref):
        def store(i, j, tile):
            ref[j, i] = tile.reshape(2, 4, 4, 8, 256)
        return store

    ring = RingZ(place, copies, 0, z_part, z_slots, z_full)
    steps = ring.scatter_steps()
    multiply(x_hi, x_lo, t_hi, t_lo, store_chunks(z_part), far)
    all_here()
    next(steps)
    fetches[2].wait()
    split_tile(1 - far)
    multiply(x_hi, x_lo, t_hi, t_lo, store_chunks(z_part), 1 - far)
    next(steps)

    @pl.loop(0, 4)
    def _(i):
        for p in (0, 1):
            rows = pl.ds(i * 128, 128)
            block = a_ref[p, :, rows].T
            lanes = slice(p * 512, (p + 1) * 512)
            xt_hi[rows, lanes], xt_lo[rows, lanes] = split(block)

    run(steps)

    def chunk_to_t(ref):
        def use(chunk):
            value = ref[chunk].reshape(64, 512)
            set_pair(pl.multiple_of(chunk * 64, 64), value[:, :256], value[:, 256:], 1.0)
        return use

    run(ring.gather_steps(chunk_to_t(z_full)))
    multiply(xt_hi, xt_lo, t_hi, t_lo, store_rows(r_part), 1 - place.core)

    def rows_to_t(k):
        @pl.loop(0, 4)
        def _(i):
            s, lines = i // 2, pl.ds(lax.rem(i, 2) * 2, 2)
            set_pair(pl.multiple_of(k * 256 + i * 64, 64), r_full[0, k, s, lines].reshape(64, 256),
                     r_full[1, k, s, lines].reshape(64, 256), -1.0)

    steps = SumRows(place, copies, Z_SLOTS, r_part, r_core, r_line, r_point, r_full).steps(rows_to_t)
    next(steps)
    multiply(xt_hi, xt_lo, t_hi, t_lo, store_rows(r_part), place.core)
    run(steps)

    ring = RingZ(place, copies, Z_SLOTS + ROW_SLOTS, z_part2, z_slots2, y_ref)
    steps = ring.scatter_steps()
    multiply(x_hi, x_lo, t_hi, t_lo, store_chunks(z_part2), far)
    next(steps)
    multiply(x_hi, x_lo, t_hi, t_lo, store_chunks(z_part2), 1 - far)
    run(steps)
    mine = z_part2[place.z].reshape(64, 512)
    steps = ring.gather_steps(chunk_to_t(y_ref))
    real, imag = mine[:, :256], mine[:, 256:]
    tall = jnp.concatenate([real, imag], 0).T
    gram_r = jnp.dot(tall, jnp.concatenate([real, imag], 0), precision=HI, preferred_element_type=F32)
    gram_i = jnp.dot(tall, jnp.concatenate([imag, -real], 0), precision=HI, preferred_element_type=F32)
    low = lax.broadcasted_iota(jnp.int32, (256, 256), 0) >= lax.broadcasted_iota(jnp.int32, (256, 256), 1)
    g_part[...] = jnp.where(low, gram_r, gram_i).reshape(2, 4, 4, 8, 256)
    gram_steps = SumAll(place, copies, 2 * Z_SLOTS + ROW_SLOTS, g_part, g_core, g_line, g_point, g_z, g_ref).steps()
    tail = SumRows(place, copies, 2 * Z_SLOTS + ROW_SLOTS + GRAM_SLOTS, r_part2, r_core2, r_line2,
                   r_point2, b_ref).steps()

    def start_b():
        multiply(xt_hi, xt_lo, t_hi, t_lo, store_rows(r_part2), 1 - place.core)
        next(tail)
        multiply(xt_hi, xt_lo, t_hi, t_lo, store_rows(r_part2), place.core)

    for turn in ORDER:
        if turn == "g":
            next(gram_steps)
        elif turn == "y":
            next(steps)
        elif turn == "b":
            start_b()
        else:
            next(tail)

    def hook(done):
        if done in HOOKS:
            next(tail)

    set_gram(g_ref[...].reshape(256, 256), m_ref)
    factor(m_ref, hook)
    run(tail)
    copies.finish()


def power(samples, sketch):
    vmem = pl.BlockSpec(memory_space=pltpu.VMEM)
    slots = 2 * Z_SLOTS + 2 * ROW_SLOTS + GRAM_SLOTS
    chunks = pltpu.VMEM((8, 4, 16, 512), F32)
    boxes = pltpu.VMEM((28, 16, 512), F32)
    rows = [
        pltpu.VMEM((2, 2, 2, 4, 4, 8, 256), F32),
        pltpu.VMEM((2, 2, 4, 4, 8, 256), F32),
        pltpu.VMEM((2, 2, 3, 4, 8, 256), F32),
        pltpu.VMEM((2, 2, 3, 8, 256), F32),
    ]
    return pl.pallas_call(
        power_kernel,
        out_shape=(
            jax.ShapeDtypeStruct((8, 4, 16, 512), F32),
            jax.ShapeDtypeStruct((2, 2, 2, 4, 4, 8, 256), F32),
            jax.ShapeDtypeStruct((512, 512), F32),
        ),
        in_specs=[pl.BlockSpec(memory_space=pl.ANY)] * 2,
        out_specs=(vmem,) * 3,
        scratch_shapes=[
            *[pltpu.VMEM((512, 1024), BF16)] * 4,
            *[pltpu.VMEM((1024, 512), BF16)] * 2,
            chunks, boxes, chunks, chunks, boxes,
            *rows, pltpu.VMEM((2, 2, 2, 4, 4, 8, 256), F32), *rows,
            *[pltpu.VMEM((2, 4, 4, 8, 256), F32)] * 2,
            pltpu.VMEM((4, 4, 8, 256), F32),
            pltpu.VMEM((3, 4, 8, 256), F32),
            pltpu.VMEM((3, 8, 256), F32),
            pltpu.VMEM((8, 8, 256), F32),
            pltpu.VMEM((2, 512, 512), F32),
            pltpu.VMEM((2, 512, 256), F32),
            pltpu.SemaphoreType.DMA((3,)),
            *[pltpu.SemaphoreType.DMA((slots,))] * 2,
        ],
        compiler_params=pltpu.CompilerParams(
            collective_id=0, has_side_effects=True, vmem_limit_bytes=50 * 2**20
        ),
        name="power",
    )(samples, sketch)


def per_device(samples, sketch):
    y, b, inverse = power(samples, sketch)
    total_rows = samples.shape[1] * lax.axis_size("rows")
    scale = float(np.sqrt(np.float32(2 * total_rows)))
    return finish(y.reshape(512, 512), b.reshape(2, 512, 256), inverse, scale)


def solution(mesh):
    placed = (P(None, "rows", "cols"), P(None, "cols", None))
    return jax.shard_map(
        per_device,
        mesh=mesh,
        in_specs=placed,
        out_specs=(P(None, "rows", None), P(None, None, "cols")),
        check_vma=False,
    )
```
